256 devices in a mesh: row: 8 (over z), col: 32 (over y, x, core).
Axes of the slice: x: 4, y: 4, z: 8, core: 2. Of those that a mesh axis runs over, the one named last changes fastest.
Arguments:
- matrix: bfloat16 [2, 8, 8, 256, 2, 32, 256], P(None, None, 'row', None, None, 'col'), may hold values from -6 to 22
- inverses: bfloat16 [2, 2, 256, 256], replicated, may hold values from -1 to 1
- pivots: int32 [2], replicated, may hold values from 0 to 63, as said below
- col_lists: int32 [2, 64], replicated, may hold values from 0 to 1
- row_lists: int32 [2, 64], replicated, may hold values from 0 to 1
Outputs:
- factored: bfloat16 [2, 8, 8, 256, 2, 32, 256], P(None, None, 'row', None, None, 'col')
The draws below stay inside these ranges and needn't reach their ends.
Inputs may be any that keep to these rules, and one draw needn't show every extreme that they name: `pivots`: two different tile indices; one of the two steps eliminates the last tile index, 63.
All inputs are finite; a program needn't handle non-finite values.
Results may differ from the reference program's by a relative error of at most 0.0037.
Values may be sent and summed in bfloat16 or wider, within the bound.
A program may use at most 128 MiB of HBM per device.

```python
import math
import jax
import jax.numpy as jnp
from jax import lax

B = 256
TC_DEV = 2
NT = 64
TR = 8
N_ROW = 8
N_COL = 32


def pivot_pair(key):
    key = jax.random.fold_in(key, 13)
    key_other, key_order = jax.random.split(key)
    other_pivot = jax.random.randint(key_other, (), 0, NT - 1).astype(jnp.int32)
    last_pivot = jnp.int32(NT - 1)
    order_bit = jax.random.randint(key_order, (), 0, 2).astype(jnp.int32)
    first_pivot = jnp.where(order_bit == 0, other_pivot, last_pivot)
    second_pivot = jnp.where(order_bit == 0, last_pivot, other_pivot)
    return jnp.stack([first_pivot, second_pivot]).astype(jnp.int32)


def fill_marks(key, fold_value):
    pair = pivot_pair(key)
    key = jax.random.fold_in(key, fold_value)
    marks = (jax.random.randint(key, (2, NT), 0, 10) < 7).astype(jnp.int32)
    step_id = lax.broadcasted_iota(jnp.int32, (2, NT), 0)
    tile_id = lax.broadcasted_iota(jnp.int32, (2, NT), 1)
    forced = (step_id == 0) & (tile_id == pair[1])
    return jnp.where(forced, 1, marks).astype(jnp.int32)


def draw_matrix(key, part):
    key = jax.random.fold_in(key, 11)
    off_scale = 5.0 / math.sqrt(2.0 * B)
    diag_scale = 2.4 / math.sqrt(2.0 * B)
    values = jnp.clip(jax.random.normal(key, (2, NT, B, NT, B), jnp.float32), -6.0, 6.0)
    tile_same = lax.broadcasted_iota(jnp.int32, (1, NT, 1, NT, 1), 1) == lax.broadcasted_iota(jnp.int32, (1, NT, 1, NT, 1), 3)
    entry_same = lax.broadcasted_iota(jnp.int32, (1, 1, B, 1, B), 2) == lax.broadcasted_iota(jnp.int32, (1, 1, B, 1, B), 4)
    real_layer = lax.broadcasted_iota(jnp.int32, (2, 1, 1, 1, 1), 0) == 0
    values = jnp.where(tile_same, diag_scale * values, off_scale * values)
    values = values + jnp.where(tile_same & entry_same & real_layer, 16.0, 0.0)
    return values.reshape(2, TR, N_ROW, B, TC_DEV, N_COL, B).astype(jnp.bfloat16)


def draw_inverses(key, part):
    key = jax.random.fold_in(key, 12)
    noise_scale = 0.0125 / math.sqrt(2.0 * B)
    values = jnp.clip(jax.random.normal(key, (2, 2, B, B), jnp.float32), -6.0, 6.0) * noise_scale
    entry_same = lax.broadcasted_iota(jnp.int32, (1, 1, B, B), 2) == lax.broadcasted_iota(jnp.int32, (1, 1, B, B), 3)
    real_layer = lax.broadcasted_iota(jnp.int32, (1, 2, 1, 1), 1) == 0
    return (values + jnp.where(entry_same & real_layer, 0.0625, 0.0)).astype(jnp.bfloat16)


def draw_pivots(key, part):
    return pivot_pair(key)


def draw_col_lists(key, part):
    return fill_marks(key, 14)


def draw_row_lists(key, part):
    return fill_marks(key, 15)


def setup_inputs(seed: int = 0) -> dict:
    streams_of = jax.random.split(jax.random.key(seed), 6)
    return {
        "matrix": draw_matrix(jax.random.fold_in(streams_of[5], 71), 0),
        "inverses": draw_inverses(jax.random.fold_in(streams_of[5], 71), 0),
        "pivots": draw_pivots(jax.random.fold_in(streams_of[5], 71), 0),
        "col_lists": draw_col_lists(jax.random.fold_in(streams_of[5], 71), 0),
        "row_lists": draw_row_lists(jax.random.fold_in(streams_of[5], 71), 0),
    }


def complex_product(left_part, right_part):
    real_real = jnp.dot(left_part[0], right_part[0], preferred_element_type=jnp.float32)
    imag_imag = jnp.dot(left_part[1], right_part[1], preferred_element_type=jnp.float32)
    real_imag = jnp.dot(left_part[0], right_part[1], preferred_element_type=jnp.float32)
    imag_real = jnp.dot(left_part[1], right_part[0], preferred_element_type=jnp.float32)
    return jnp.stack([real_real - imag_imag, real_imag + imag_real])


def refine(diagonal, guess_inv):
    product = complex_product(diagonal, guess_inv)
    identity = jnp.eye(diagonal.shape[1], dtype=jnp.float32)
    residue = jnp.stack([2.0 * identity - product[0], -product[1]]).astype(jnp.bfloat16)
    return complex_product(guess_inv, residue).astype(jnp.bfloat16)


def reference(matrix, inverses, pivots, col_lists, row_lists):
    total = NT * B
    whole = matrix.reshape(2, total, total)
    first_pivot = pivots[0]
    tile_ids = jnp.arange(NT, dtype=jnp.int32)
    for step_no in range(2):
        pivot_id = pivots[step_no].astype(jnp.int32)
        live = tile_ids != pivot_id
        if step_no == 1:
            live = live & (tile_ids != first_pivot)
        take_rows = (col_lists[step_no] > 0) & live
        take_cols = (row_lists[step_no] > 0) & live
        start_p = (pivot_id * B).astype(jnp.int32)
        zero_idx = jnp.int32(0)
        diagonal = lax.dynamic_slice(whole, (zero_idx, start_p, start_p), (2, B, B))
        factor = refine(diagonal, inverses[step_no])

        def eliminate(index, current):
            row_start = (index * B).astype(jnp.int32)
            this_tile = lax.dynamic_slice(current, (zero_idx, row_start, start_p), (2, B, B))
            new_tile = lax.cond(take_rows[index], lambda: complex_product(this_tile, factor).astype(jnp.bfloat16), lambda: this_tile)
            return lax.dynamic_update_slice(current, new_tile, (zero_idx, row_start, start_p))

        whole = lax.fori_loop(0, NT, eliminate, whole)
        whole = lax.dynamic_update_slice(whole, factor, (zero_idx, start_p, start_p))

        def update(index, current):
            row_id = (index // NT).astype(jnp.int32)
            col_id = (index % NT).astype(jnp.int32)
            row_start = row_id * B
            col_start = col_id * B
            this_tile = lax.dynamic_slice(current, (zero_idx, row_start, col_start), (2, B, B))
            left_tile = lax.dynamic_slice(current, (zero_idx, row_start, start_p), (2, B, B))
            right_tile = lax.dynamic_slice(current, (zero_idx, start_p, col_start), (2, B, B))
            new_tile = lax.cond(take_rows[row_id] & take_cols[col_id], lambda: (this_tile.astype(jnp.float32) - complex_product(left_tile, right_tile)).astype(jnp.bfloat16), lambda: this_tile)
            return lax.dynamic_update_slice(current, new_tile, (zero_idx, row_start, col_start))

        whole = lax.fori_loop(0, NT * NT, update, whole)
    return whole.reshape(matrix.shape)
```

```python
import functools

import jax
import jax.numpy as jnp
from jax import lax
from jax.experimental import pallas as pl
from jax.experimental.pallas import tpu as pltpu
from jax.sharding import PartitionSpec as P

MESH = pl.DeviceIdType.MESH
B = 256
NX = 4
NY = 4
NZ = 8
DIRS = ((1, 0), (0, 1), (-1, 0), (0, -1))
PARENT = {
    (1, 0): 0, (0, 1): 2, (3, 0): 0, (0, 3): 2, (1, 1): 1, (3, 1): 0, (3, 3): 0, (1, 3): 3,
    (1, 2): 1, (2, 1): 0, (3, 2): 0, (2, 3): 3, (2, 0): 0, (0, 2): 2, (2, 2): 0,
}
STEPS = 18


def turn(v, k):
    x, y = v
    for _ in range(k % 4):
        x, y = (-y) % 4, x % 4
    return x, y


def tree_tables():
    depth0 = {(0, 0): 0}
    while len(depth0) < 16:
        for v, d in PARENT.items():
            up = ((v[0] - DIRS[d][0]) % 4, (v[1] - DIRS[d][1]) % 4)
            if up in depth0:
                depth0[v] = depth0[up] + 1
    depth = [[0] * 16 for _ in range(4)]
    sends = [[[0] * 16 for _ in range(4)] for _ in range(4)]
    for k in range(4):
        for v, d in PARENT.items():
            w = turn(v, k)
            depth[k][w[1] * 4 + w[0]] = depth0[v]
            e = (d + k) % 4
            up = ((w[0] - DIRS[e][0]) % 4, (w[1] - DIRS[e][1]) % 4)
            sends[k][e][up[1] * 4 + up[0]] = 1
    return depth, sends


DEPTH, SENDS = tree_tables()


def bits(flags):
    return sum(1 << i for i, f in enumerate(flags) if f)


def pick(table, idx):
    total = jnp.int32(0)
    for level in range(1, max(table) + 1):
        total = total + ((jnp.int32(bits([v >= level for v in table])) >> idx) & 1)
    return total


def gather_kernel(pivot_col, col_ref, row_ref, cor_ref, x_ref, u_ref, rx, rd, rz, ru, sx, sd, sz, su, loc):
    z = lax.axis_index("row")
    c = lax.axis_index("col")
    y, x, core = c // 8, (c // 2) % 4, c % 2
    cols = (pivot_col, 31)
    rows = (pivot_col % 8, 7)

    def dev(dz, dy, dx, to_core):
        return ((z + dz + 8) % 8, ((y + dy + 4) % 4) * 8 + ((x + dx + 4) % 4) * 2 + to_core)

    bar = pltpu.get_barrier_semaphore()
    greet = [dev(0, dy, dx, k) for dx, dy in DIRS for k in range(2)]
    greet += [dev(1, 0, 0, core), dev(-1, 0, 0, core), dev(0, 0, 0, 1 - core)]
    for d in greet:
        pl.semaphore_signal(bar, inc=1, device_id=d, device_id_type=MESH)
    pl.semaphore_wait(bar, len(greet))

    def remote(src, dst, ssem, rsem, to):
        return pltpu.make_async_remote_copy(
            src_ref=src, dst_ref=dst, send_sem=ssem, recv_sem=rsem, device_id=to, device_id_type=MESH
        )

    own = [c == cols[b] for b in range(2)]
    rel = []
    for b in range(2):
        yb, xb = cols[b] // 8, (cols[b] // 2) % 4
        rel.append(((y - yb + 4) % 4) * 4 + (x - xb + 4) % 4)
    tree = [core, core + 2]
    deep = [[jnp.where(core == 0, pick(DEPTH[2 * i], rel[b]), pick(DEPTH[2 * i + 1], rel[b])) for i in range(2)] for b in range(2)]
    fwd = [
        [
            [jnp.where(core == 0, pick(SENDS[2 * i][d], rel[b]), pick(SENDS[2 * i + 1][d], rel[b])) for d in range(4)]
            for i in range(2)
        ]
        for b in range(2)
    ]
    right = [(z - rows[a] + 8) % 8 for a in range(2)]
    hop = [jnp.where(right[a] <= 4, right[a], 8 - right[a]) for a in range(2)]
    on_right = [(right[a] >= 1) & (right[a] <= 4) for a in range(2)]
    go_right = [right[a] <= 3 for a in range(2)]
    go_left = [(right[a] == 0) | (right[a] >= 6) for a in range(2)]

    to_right = dev(1, 0, 0, core)
    to_left = dev(-1, 0, 0, core)
    sibling = dev(0, 0, 0, 1 - core)

    for b in range(2):
        @pl.when(own[b])
        def _(b=b):
            for j in range(4):
                for k in range(4):
                    dx, dy = DIRS[k]
                    remote(col_ref.at[b, k, j], x_ref.at[b, k, j], sx.at[b, k], rx.at[b, k, j], dev(0, dy, dx, k % 2)).start()

    for b in range(2):
        for a in range(2):
            @pl.when(own[b] & (right[a] == 0))
            def _(a=a, b=b):
                src = cor_ref.at[b, pl.ds(2 * a, 2)]
                dst = x_ref.at[b, pl.ds(2 * a, 2), 4]
                remote(src, dst, sz.at[b, a, 0], rz.at[b, a], to_right).start()
                remote(src, dst, sz.at[b, a, 1], rz.at[b, a], to_left).start()
                pltpu.make_async_copy(src, dst, rz.at[b, a]).start()

    for a in range(2):
        @pl.when(right[a] == 0)
        def _(a=a):
            for u in range(4):
                remote(row_ref.at[a, u], u_ref.at[a, u], su.at[a, 0], ru.at[a, u], to_right).start()
                remote(row_ref.at[a, u], u_ref.at[a, u], su.at[a, 1], ru.at[a, u], to_left).start()
            pltpu.make_async_copy(row_ref.at[a], u_ref.at[a], loc.at[2 + a]).start()

    for b in range(2):
        @pl.when(own[b])
        def _(b=b):
            for k in range(4):
                remote(col_ref.at[b, k], x_ref.at[b, k, pl.ds(0, 4)], sd.at[b, k], rd.at[b, k], sibling).start()
            pltpu.make_async_copy(col_ref.at[b], x_ref.at[b, :, pl.ds(0, 4)], loc.at[b]).start()

    def forward(b, i, k, j):
        part = x_ref.at[b, k, j]
        for d, (dx, dy) in enumerate(DIRS):
            @pl.when(fwd[b][i][d] == 1)
            def _(d=d, dx=dx, dy=dy):
                remote(part, part, sx.at[b, d], rx.at[b, k, j], dev(0, dy, dx, core)).start()
        remote(part, part, sd.at[b, k], rd.at[b, k], sibling).start()

    def step(t, carry):
        for b in range(2):
            for a in range(2):
                @pl.when(own[b] & (t == 2 * hop[a]))
                def _(a=a, b=b):
                    part = x_ref.at[b, pl.ds(2 * a, 2), 4]
                    remote(part, part, sz.at[b, a, 0], rz.at[b, a], to_right).wait_recv()

                    @pl.when(go_right[a] & (hop[a] > 0))
                    def _():
                        remote(part, part, sz.at[b, a, 0], rz.at[b, a], to_right).start()

                    @pl.when(go_left[a] & (hop[a] > 0))
                    def _():
                        remote(part, part, sz.at[b, a, 1], rz.at[b, a], to_left).start()

                    for r in range(2):
                        k = 2 * a + r
                        dx, dy = DIRS[k]
                        unit = x_ref.at[b, k, 4]
                        remote(unit, unit, sx.at[b, k], rx.at[b, k, 4], dev(0, dy, dx, k % 2)).start()
                        remote(unit, unit, sd.at[b, k], rd.at[b, k], sibling).start()
        for b in range(2):
            for i in range(2):
                j = t - 2 * deep[b][i] + 1

                @pl.when((deep[b][i] > 0) & (j >= 0) & (j < 4))
                def _(b=b, i=i, j=j):
                    k = tree[i]
                    part = x_ref.at[b, k, j]
                    remote(part, part, sx.at[b, 0], rx.at[b, k, j], sibling).wait_recv()
                    forward(b, i, k, j)
        for a in range(2):
            u = t - 2 * hop[a]

            @pl.when((hop[a] > 0) & (u >= 0) & (u < 4))
            def _(a=a, u=u):
                part = u_ref.at[a, u]
                remote(part, part, su.at[a, 0], ru.at[a, u], to_right).wait_recv()

                @pl.when(go_right[a])
                def _():
                    remote(part, part, su.at[a, 0], ru.at[a, u], to_right).start()

                @pl.when(go_left[a])
                def _():
                    remote(part, part, su.at[a, 1], ru.at[a, u], to_left).start()
        for b in range(2):
            for i in range(2):
                at = jnp.maximum(4, 2 * hop[i] + 1) + 2 * deep[b][i] - 1

                @pl.when((deep[b][i] > 0) & (t == at))
                def _(b=b, i=i):
                    k = tree[i]
                    part = x_ref.at[b, k, 4]
                    remote(part, part, sx.at[b, 0], rx.at[b, k, 4], sibling).wait_recv()
                    forward(b, i, k, 4)
        return carry

    lax.fori_loop(0, STEPS + 2, step, 0)

    for b in range(2):
        home = rel[b] == 0
        for k in range(4):
            whole = x_ref.at[b, k]

            @pl.when(own[b])
            def _(b=b, k=k, whole=whole):
                remote(whole, whole, sx.at[b, k], rd.at[b, k], sibling).wait_send()
                remote(whole, whole, sd.at[b, k], rd.at[b, k], sibling).wait_send()

            @pl.when((home & jnp.logical_not(own[b])) | (jnp.logical_not(home) & (core != k % 2)))
            def _(b=b, k=k, whole=whole):
                remote(whole, whole, sx.at[b, k], rd.at[b, k], sibling).wait_recv()

            @pl.when(jnp.logical_not(home) & (core == k % 2))
            def _(b=b, k=k, whole=whole):
                remote(whole, whole, sd.at[b, k], rd.at[b, k], sibling).wait_send()

        for i in range(2):
            whole = x_ref.at[b, tree[i]]
            for d in range(4):
                @pl.when(jnp.logical_not(home) & (fwd[b][i][d] == 1))
                def _(b=b, d=d, whole=whole):
                    remote(whole, whole, sx.at[b, d], rd.at[b, 0], sibling).wait_send()

        @pl.when(own[b])
        def _(b=b):
            pltpu.make_async_copy(col_ref.at[b], x_ref.at[b, :, pl.ds(0, 4)], loc.at[b]).wait()
            for a in range(2):
                part = x_ref.at[b, pl.ds(2 * a, 2), 4]

                @pl.when(go_right[a])
                def _(a=a, part=part):
                    remote(part, part, sz.at[b, a, 0], rz.at[b, a], to_right).wait_send()

                @pl.when(go_left[a])
                def _(a=a, part=part):
                    remote(part, part, sz.at[b, a, 1], rz.at[b, a], to_left).wait_send()

    for a in range(2):
        whole = u_ref.at[a]

        @pl.when(right[a] == 0)
        def _(a=a, whole=whole):
            pltpu.make_async_copy(row_ref.at[a], whole, loc.at[2 + a]).wait()

        @pl.when(go_right[a])
        def _(a=a, whole=whole):
            remote(whole, whole, su.at[a, 0], ru.at[a, 0], to_right).wait_send()

        @pl.when(go_left[a])
        def _(a=a, whole=whole):
            remote(whole, whole, su.at[a, 1], ru.at[a, 0], to_left).wait_send()


def gather(pivot_col, cols, rows, corners):
    dma = pltpu.SemaphoreType.DMA
    anywhere = pl.BlockSpec(memory_space=pl.ANY)
    return pl.pallas_call(
        functools.partial(gather_kernel, pivot_col),
        name=f"gather_{pivot_col}",
        out_shape=[
            jax.ShapeDtypeStruct((2, 4, 5, B, B), jnp.bfloat16),
            jax.ShapeDtypeStruct((2, 4, B, B), jnp.bfloat16),
        ],
        in_specs=[anywhere] * 3,
        out_specs=[anywhere] * 2,
        scratch_shapes=[
            dma((2, 4, 5)), dma((2, 4)), dma((2, 2)), dma((2, 4)),
            dma((2, 4)), dma((2, 4)), dma((2, 2, 2)), dma((2, 2)), dma((4,)),
        ],
        compiler_params=pltpu.CompilerParams(collective_id=pivot_col, has_side_effects=True),
    )(cols, rows, corners)


def mult(left, right):
    return jnp.einsum("...ik,...kn->...in", left, right, preferred_element_type=jnp.float32)


def cmul(left, right):
    real = mult(left[0], right[0]) - mult(left[1], right[1])
    imag = mult(left[0], right[1]) + mult(left[1], right[0])
    return jnp.stack([real, imag])


def refine(diagonal, guess_inv):
    product = cmul(diagonal, guess_inv)
    identity = jnp.eye(B, dtype=jnp.float32)
    residue = jnp.stack([2.0 * identity - product[0], -product[1]]).astype(jnp.bfloat16)
    return cmul(guess_inv, residue).astype(jnp.bfloat16)


def shards(matrix, inverses, pivots, col_lists, row_lists):
    f32, bf = jnp.float32, jnp.bfloat16
    z = lax.axis_index("row")
    c = lax.axis_index("col")
    tiles = matrix.reshape(2, 8, B, 2, B).transpose(0, 1, 3, 2, 4)
    first_last = pivots[0] == 63
    other = jnp.where(first_last, pivots[1], pivots[0])
    ids = (other, jnp.int32(63))
    cols = [lax.dynamic_index_in_dim(tiles, ids[b] // 32, 2, keepdims=False) for b in range(2)]
    rows = [lax.dynamic_index_in_dim(tiles, ids[a] // 8, 1, keepdims=False) for a in range(2)]
    corners = [
        jnp.stack([lax.dynamic_index_in_dim(cols[b], ids[a] // 8, 1, keepdims=False) for a in range(2)])
        for b in range(2)
    ]
    col_in = jnp.stack([q.reshape(4, 4, B, B).transpose(1, 0, 2, 3) for q in cols])
    row_in = jnp.stack([q.reshape(4, B, B) for q in rows])
    cor_in = jnp.stack([q.reshape(4, B, B) for q in corners])
    x_out, u_out = lax.switch(
        other % 32, [functools.partial(gather, q) for q in range(32)], col_in, row_in, cor_in
    )
    order = jnp.where(first_last, jnp.array([1, 0]), jnp.array([0, 1]))
    panel = jnp.stack([x_out[order[s], :, :4].transpose(1, 0, 2, 3).reshape(2, 8, B, B) for s in range(2)])
    upper = jnp.stack([u_out[order[s]].reshape(2, 2, B, B) for s in range(2)])
    corner = jnp.stack(
        [jnp.stack([x_out[order[t], :, 4].reshape(2, 2, B, B)[order[s]] for t in range(2)]) for s in range(2)]
    )
    row_ids = jnp.arange(8) * 8 + z
    col_ids = jnp.arange(2) * 32 + c
    p0, p1 = pivots[0], pivots[1]
    take_r = [(col_lists[0][row_ids] > 0) & (row_ids != p0), (col_lists[1][row_ids] > 0) & (row_ids != p1) & (row_ids != p0)]
    take_c = [(row_lists[0][col_ids] > 0) & (col_ids != p0), (row_lists[1][col_ids] > 0) & (col_ids != p1) & (col_ids != p0)]
    x0 = refine(corner[0, 0], inverses[0])
    l10 = cmul(corner[1, 0], x0).astype(bf)
    corner01 = corner[0, 1]
    m11 = (corner[1, 1].astype(f32) - cmul(l10, corner01)).astype(bf)
    x1 = refine(m11, inverses[1])
    l0 = cmul(panel[0], x0[:, None]).astype(bf)
    l0m = jnp.where(take_r[0][None, :, None, None], l0, panel[0])
    c1 = (panel[1].astype(f32) - cmul(l0, corner01[:, None])).astype(bf)
    c1 = jnp.where(take_r[0][None, :, None, None], c1, panel[1])
    c1 = jnp.where((row_ids == p0)[None, :, None, None], corner01[:, None], c1)
    l1 = cmul(c1, x1[:, None]).astype(bf)
    l1m = jnp.where(take_r[1][None, :, None, None], l1, c1)
    u1 = (upper[1].astype(f32) - cmul(l10[:, None], upper[0])).astype(bf)
    u1 = jnp.where(take_c[0][None, :, None, None], u1, upper[1])
    u1 = jnp.where((col_ids == p0)[None, :, None, None], l10[:, None], u1)
    now = tiles
    for s, (l, u, pid, x) in enumerate(((l0m, upper[0], p0, x0), (l1m, u1, p1, x1))):
        new = (now.astype(f32) - cmul(l[:, :, None], u[:, None])).astype(bf)
        now = jnp.where((take_r[s][:, None] & take_c[s][None, :])[None, :, :, None, None], new, now)
        here = (col_ids == pid)[None, None, :, None, None]
        now = jnp.where(here, l[:, :, None], now)
        now = jnp.where(here & (row_ids == pid)[None, :, None, None, None], x[:, None, None], now)
    return now.transpose(0, 1, 3, 2, 4).reshape(matrix.shape)


def solution(mesh):
    tiled = P(None, None, "row", None, None, "col", None)
    return jax.shard_map(shards, mesh=mesh, in_specs=(tiled, P(), P(), P(), P()), out_specs=tiled, check_vma=False)
```

```python
import jax
import jax.numpy as jnp
from jax import lax
from jax.experimental import pallas as pl
from jax.experimental.pallas import tpu as pltpu
from jax.sharding import PartitionSpec as P

MESH = pl.DeviceIdType.MESH
B = 256
HALF = 128
SLAB = 32


def gather_kernel(
    piv_ref, colq, col63, rowq, row63, xbuf, ubuf, kbuf,
    other_q, picked, from_chips, other_63, xown, from_rows, uown, mine_c, other_c, picked_c, from_chips_c, kown,
    s_half, s_col, s_col63, s_all, s_row, s_row63, s_urow, s_cor, s_ccol, s_ccol63, s_krow, s_xsib, s_ksib,
    r_half, r_col, r_col63, r_all, r_row, r_row63, r_urow, r_cor, r_ccol, r_ccol63, r_krow, r_xsib, r_ksib,
):
    z = lax.axis_index("row")
    c = lax.axis_index("col")
    chip, core = c // 2, c % 2
    last_chip = chip == 15
    q = jnp.where(piv_ref[0] == 63, piv_ref[1], piv_ref[0])
    q_row, q_chip, q_core = q % 8, (q % 32) // 2, q % 2
    q_here = q_core == core
    sibling = (z, chip * 2 + 1 - core)

    def to_chip(step):
        return lax.rem(chip + step, 16)

    def to_row(step):
        return lax.rem(z + step, 8)

    def remote(src, dst, ssem, rsem, to):
        return pltpu.make_async_remote_copy(
            src_ref=src, dst_ref=dst, send_sem=ssem, recv_sem=rsem, device_id=to, device_id_type=MESH
        )

    def on_chip(p):
        return (z, p * 2 + core)

    def on_row(w):
        return (w, c)

    bar = pltpu.get_barrier_semaphore()

    def greet_chip(i, carry):
        pl.semaphore_signal(bar, inc=1, device_id=on_chip(to_chip(i)), device_id_type=MESH)
        return carry

    def greet_row(i, carry):
        pl.semaphore_signal(bar, inc=1, device_id=on_row(to_row(i)), device_id_type=MESH)
        return carry

    lax.fori_loop(1, 16, greet_chip, 0)
    lax.fori_loop(1, 8, greet_row, 0)
    pl.semaphore_signal(bar, inc=1, device_id=sibling, device_id_type=MESH)
    pl.semaphore_wait(bar, 23)

    half_q = remote(colq.at[:, 1 - core], other_q, s_half.at[0], r_half.at[0], sibling)
    half_63 = remote(col63.at[:, 0], other_63, s_half.at[1], r_half.at[1], sibling)
    half_q.start()

    @pl.when(last_chip & (core == 1))
    def _():
        half_63.start()

    def send_row(i, carry):
        w = to_row(i)
        remote(rowq.at[w], from_rows.at[z], s_row.at[i], r_row.at[z], on_row(w)).start()

        @pl.when(z == 7)
        def _():
            remote(row63.at[w], uown.at[1], s_row63.at[i], r_row63.at[0], on_row(w)).start()
        return carry

    lax.fori_loop(1, 8, send_row, 0)

    half_q.wait_recv()

    def pick(i, carry):
        picked[i] = jnp.where(q_here, colq[i, core], other_q[i])
        return carry

    lax.fori_loop(0, 16, pick, 0)

    @pl.when(last_chip & (core == 0))
    def _():
        half_63.wait_recv()

    def send_col(i, carry):
        p = to_chip(i)
        remote(picked.at[p], from_chips.at[chip], s_col.at[i], r_col.at[chip], on_chip(p)).start()

        @pl.when(last_chip & (core == 0))
        def _():
            remote(other_63.at[p], xown.at[1], s_col63.at[i], r_col63.at[0], on_chip(p)).start()

        @pl.when(last_chip & (core == 1))
        def _():
            remote(col63.at[p, 1], xown.at[1], s_col63.at[i], r_col63.at[0], on_chip(p)).start()
        return carry

    lax.fori_loop(1, 16, send_col, 0)
    from_chips[chip] = picked[chip]

    @pl.when(last_chip)
    def _():
        xown[1] = jnp.where(core == 0, other_63[15], col63[15, 1])

    from_rows[z] = rowq[z]

    @pl.when(z == 7)
    def _():
        uown[1] = row63[7]

    def wait_row(i, carry):
        w = to_row(i)
        remote(from_rows.at[w], from_rows.at[w], s_row.at[i], r_row.at[w], on_row(w)).wait_recv()
        return carry

    lax.fori_loop(1, 8, wait_row, 0)
    uown[0] = from_rows[q_row]

    @pl.when(z != 7)
    def _():
        remote(uown.at[1], uown.at[1], s_row63.at[0], r_row63.at[0], on_row(z)).wait_recv()

    q_tc = q // 32
    for a in range(2):
        for r in range(2):
            mine_c[0, a, r] = uown[a, 2 * q_tc + r]
            mine_c[1, a, r] = uown[a, 2 + r]
    cor_q = remote(mine_c.at[0, 1 - core], other_c.at[0], s_cor.at[0], r_cor.at[0], sibling)
    cor_63 = remote(mine_c.at[1, 0], other_c.at[1], s_cor.at[1], r_cor.at[1], sibling)
    cor_q.start()

    @pl.when(last_chip & (core == 1))
    def _():
        cor_63.start()

    def send_urow(i, carry):
        remote(uown, ubuf.at[z], s_urow.at[i], r_urow.at[z], on_row(to_row(i))).start()
        return carry

    lax.fori_loop(1, 8, send_urow, 0)
    ubuf[z] = uown[...]

    cor_q.wait_recv()
    picked_c[0] = jnp.where(q_here, mine_c[0, core], other_c[0])

    @pl.when(last_chip & (core == 0))
    def _():
        cor_63.wait_recv()
        kown[1] = other_c[1]

    @pl.when(last_chip & (core == 1))
    def _():
        kown[1] = mine_c[1, 1]

    def send_ccol(i, carry):
        p = to_chip(i)
        remote(picked_c.at[0], from_chips_c.at[chip], s_ccol.at[i], r_ccol.at[chip], on_chip(p)).start()

        @pl.when(last_chip)
        def _():
            remote(kown.at[1], kown.at[1], s_ccol63.at[i], r_ccol63.at[0], on_chip(p)).start()
        return carry

    lax.fori_loop(1, 16, send_ccol, 0)
    from_chips_c[chip] = picked_c[0]

    def wait_col(i, carry):
        p = to_chip(i)
        remote(from_chips.at[p], from_chips.at[p], s_col.at[i], r_col.at[p], on_chip(p)).wait_recv()
        return carry

    lax.fori_loop(1, 16, wait_col, 0)
    xown[0] = from_chips[q_chip]

    @pl.when(jnp.logical_not(last_chip))
    def _():
        remote(xown.at[1], xown.at[1], s_col63.at[0], r_col63.at[0], sibling).wait_recv()

    def send_all(i, carry):
        remote(xown, xbuf.at[core, chip], s_all.at[i], r_all.at[chip], on_chip(to_chip(i))).start()
        return carry

    lax.fori_loop(1, 16, send_all, 0)
    xbuf[core, chip] = xown[...]

    def wait_ccol(i, carry):
        p = to_chip(i)
        remote(picked_c.at[0], from_chips_c.at[p], s_ccol.at[i], r_ccol.at[p], on_chip(p)).wait_recv()
        return carry

    lax.fori_loop(1, 16, wait_ccol, 0)
    kown[0] = from_chips_c[q_chip]

    @pl.when(jnp.logical_not(last_chip))
    def _():
        remote(kown.at[1], kown.at[1], s_ccol63.at[0], r_ccol63.at[0], sibling).wait_recv()

    def send_krow(i, carry):
        remote(kown, kbuf.at[core, z], s_krow.at[i], r_krow.at[z], on_row(to_row(i))).start()
        return carry

    lax.fori_loop(1, 8, send_krow, 0)
    kbuf[core, z] = kown[...]

    for part in range(4):
        for i in range(4 * part, 4 * part + 4):
            @pl.when(chip != i)
            def _(i=i):
                remote(xown, xbuf.at[core, i], s_all.at[0], r_all.at[i], sibling).wait_recv()
        block = xbuf.at[core, pl.ds(4 * part, 4)]
        remote(block, block, s_xsib.at[part], r_xsib.at[part], sibling).start()

    def wait_krow(i, carry):
        w = to_row(i)
        remote(kown, kbuf.at[core, w], s_krow.at[i], r_krow.at[w], on_row(w)).wait_recv()
        return carry

    lax.fori_loop(1, 8, wait_krow, 0)
    both = remote(kbuf.at[core], kbuf.at[core], s_ksib.at[0], r_ksib.at[0], sibling)
    both.start()

    def wait_urow(i, carry):
        w = to_row(i)
        remote(uown, ubuf.at[w], s_urow.at[i], r_urow.at[w], on_row(w)).wait_recv()
        return carry

    lax.fori_loop(1, 8, wait_urow, 0)

    half_q.wait_send()
    cor_q.wait_send()

    @pl.when(last_chip & (core == 1))
    def _():
        half_63.wait_send()
        cor_63.wait_send()

    def sent_rows(i, carry):
        to = on_row(to_row(i))
        remote(rowq.at[0], from_rows.at[0], s_row.at[i], r_row.at[0], to).wait_send()
        remote(uown, ubuf.at[0], s_urow.at[i], r_urow.at[0], to).wait_send()
        remote(kown, kbuf.at[0, 0], s_krow.at[i], r_krow.at[0], to).wait_send()

        @pl.when(z == 7)
        def _():
            remote(row63.at[0], uown.at[1], s_row63.at[i], r_row63.at[0], to).wait_send()
        return carry

    lax.fori_loop(1, 8, sent_rows, 0)

    def sent_chips(i, carry):
        to = on_chip(to_chip(i))
        remote(picked.at[0], from_chips.at[0], s_col.at[i], r_col.at[0], to).wait_send()
        remote(xown, xbuf.at[0, 0], s_all.at[i], r_all.at[0], to).wait_send()
        remote(picked_c.at[0], from_chips_c.at[0], s_ccol.at[i], r_ccol.at[0], to).wait_send()

        @pl.when(last_chip)
        def _():
            remote(picked.at[0], xown.at[1], s_col63.at[i], r_col63.at[0], to).wait_send()
            remote(kown.at[1], kown.at[1], s_ccol63.at[i], r_ccol63.at[0], to).wait_send()
        return carry

    lax.fori_loop(1, 16, sent_chips, 0)
    for part in range(4):
        block = xbuf.at[1 - core, pl.ds(4 * part, 4)]
        remote(block, block, s_xsib.at[part], r_xsib.at[part], sibling).wait()
    both.wait_send()
    remote(kbuf.at[1 - core], kbuf.at[1 - core], s_ksib.at[0], r_ksib.at[0], sibling).wait_recv()


def gather(pivots, colq, col63, rowq, row63):
    bf = jnp.bfloat16
    shape = jax.ShapeDtypeStruct
    vmem = pl.BlockSpec(memory_space=pltpu.VMEM)
    dma = pltpu.SemaphoreType.DMA
    sems = [dma((n,)) for n in (2, 16, 16, 16, 8, 8, 8, 2, 16, 16, 8, 4, 1)]
    return pl.pallas_call(
        gather_kernel,
        name="gather_0",
        out_shape=[
            shape((2, 16, 2, HALF, B), bf),
            shape((8, 2, 4, SLAB, B), bf),
            shape((2, 8, 2, 2, SLAB, B), bf),
        ],
        in_specs=[pl.BlockSpec(memory_space=pltpu.SMEM)] + [vmem] * 4,
        out_specs=[vmem] * 3,
        scratch_shapes=[
            pltpu.VMEM((16, HALF, B), bf), pltpu.VMEM((16, HALF, B), bf), pltpu.VMEM((16, HALF, B), bf),
            pltpu.VMEM((16, HALF, B), bf), pltpu.VMEM((2, HALF, B), bf),
            pltpu.VMEM((8, 4, SLAB, B), bf), pltpu.VMEM((2, 4, SLAB, B), bf),
            pltpu.VMEM((2, 2, 2, SLAB, B), bf), pltpu.VMEM((2, 2, SLAB, B), bf),
            pltpu.VMEM((1, 2, SLAB, B), bf), pltpu.VMEM((16, 2, SLAB, B), bf), pltpu.VMEM((2, 2, SLAB, B), bf),
        ] + sems + sems,
        compiler_params=pltpu.CompilerParams(collective_id=0, has_side_effects=True, vmem_limit_bytes=24 * 2**20),
    )(pivots, colq, col63, rowq, row63)


def split_kernel(piv_ref, m_ref, d_ref, colq_ref, col63_ref, rowq_ref, row63_ref):
    group = pl.program_id(0)
    other = jnp.where(piv_ref[0] == 63, piv_ref[1], piv_ref[0])
    out_row = lax.broadcasted_iota(jnp.int32, (B, B), 0)
    in_row = lax.broadcasted_iota(jnp.int32, (B, B), 1)
    perm = jnp.where(in_row == (out_row % 64) * 4 + out_row // 64, 1.0, 0.0).astype(jnp.bfloat16)
    for r in range(2):
        for t in range(2):
            j = 2 * r + t
            for half in range(2):
                pair = jnp.concatenate([m_ref[r, t, pl.ds((2 * half + s) * B, B), :] for s in range(2)], axis=1)
                sorted_rows = jnp.dot(perm, pair, preferred_element_type=jnp.float32).astype(jnp.bfloat16)
                for s in range(2):
                    for lb in range(2):
                        for tc in range(2):
                            piece = sorted_rows[(lb * 2 + tc) * 64:(lb * 2 + tc + 1) * 64, s * 128:(s + 1) * 128]
                            here = (pl.ds((2 * half + s) * 64, 64), pl.ds(lb * 128, 128))
                            d_ref[(tc, group, j, *here)] = piece

            for h in range(2):
                rows = pl.ds(h * HALF, HALF)
                colq_ref[8 * r + 2 * group + t, h] = d_ref[other // 32, group, j, rows]
                col63_ref[8 * r + 2 * group + t, h] = d_ref[1, group, j, rows]

            @pl.when(other // 8 == 2 * group + t)
            def _(r=r, j=j):
                for tc in range(2):
                    for w in range(8):
                        rowq_ref[w, 2 * tc + r] = d_ref[tc, group, j, pl.ds(w * SLAB, SLAB)]

            if t == 1:
                @pl.when(group == 3)
                def _(r=r, j=j):
                    for tc in range(2):
                        for w in range(8):
                            row63_ref[w, 2 * tc + r] = d_ref[tc, group, j, pl.ds(w * SLAB, SLAB)]


def split(pivots, packed):
    shape = jax.ShapeDtypeStruct
    vmem = pl.BlockSpec(memory_space=pltpu.VMEM)
    return pl.pallas_call(
        split_kernel,
        name="split",
        grid=(4,),
        out_shape=[
            shape((2, 4, 4, B, B), jnp.bfloat16),
            shape((16, 2, HALF, B), jnp.bfloat16),
            shape((16, 2, HALF, B), jnp.bfloat16),
            shape((8, 4, SLAB, B), jnp.bfloat16),
            shape((8, 4, SLAB, B), jnp.bfloat16),
        ],
        in_specs=[
            pl.BlockSpec(memory_space=pltpu.SMEM),
            pl.BlockSpec((2, 2, 4 * B, 128), lambda g: (0, g, 0, 0)),
        ],
        out_specs=[vmem] * 5,
        compiler_params=pltpu.CompilerParams(vmem_limit_bytes=24 * 2**20),
    )(pivots, packed)


def dot(left, right):
    return jnp.dot(left, right, preferred_element_type=jnp.float32)


def flat(pair):
    return jnp.concatenate([pair[0], pair[1]], axis=1)


def store_right(ref, pair, at=0, width=B):
    ref[pl.ds(0, B), pl.ds(at, B)] = pair[0]
    ref[pl.ds(B, B), pl.ds(at, B)] = -pair[1]
    ref[pl.ds(0, B), pl.ds(at + width, B)] = pair[1]
    ref[pl.ds(B, B), pl.ds(at + width, B)] = pair[0]


def halves(wide):
    return wide[:, :B], wide[:, B:]


def update_kernel(
    piv_ref, cl_ref, rl_ref, inv_ref, x_ref, u_ref, k_ref, d_ref, o_ref,
    f0, f1, rx0, rx1, rm01, ru0, ru1, tmp, l0, l1, tile,
):
    bf, f32 = jnp.bfloat16, jnp.float32
    group = pl.program_id(0)
    z = lax.axis_index("row")
    c = lax.axis_index("col")
    p0, p1 = piv_ref[0], piv_ref[1]
    s0 = jnp.where(p0 == 63, 1, 0)
    s1 = 1 - s0
    col_ids = [tc * 32 + c for tc in range(2)]
    cols0 = [(rl_ref[0, i] > 0) & (i != p0) for i in col_ids]
    cols1 = [(rl_ref[1, i] > 0) & (i != p0) & (i != p1) for i in col_ids]

    def from_column(s, r, row):
        return jnp.concatenate([x_ref[h, 8 * r + row, s] for h in range(2)], axis=0)

    def from_row(s, at):
        return jnp.concatenate([u_ref[w, s, at] for w in range(8)], axis=0)

    def corner(row, col):
        return [jnp.concatenate([k_ref[row, w, col, r] for w in range(8)], axis=0) for r in range(2)]

    def taken(row):
        return (cl_ref[0, row] > 0) & (row != p0), (cl_ref[1, row] > 0) & (row != p0) & (row != p1)

    @pl.when(group == 0)
    def _():
        def refine(diagonal, step, keep, keep_right):
            guess = (inv_ref[step, 0], inv_ref[step, 1])
            store_right(tmp, guess)
            eye = lax.broadcasted_iota(jnp.int32, (B, B), 0) == lax.broadcasted_iota(jnp.int32, (B, B), 1)
            real, imag = halves(dot(diagonal, tmp[...]))
            store_right(tmp, ((jnp.where(eye, 2.0, 0.0) - real).astype(bf), (-imag).astype(bf)))
            keep[...] = dot(flat(guess), tmp[...]).astype(bf)
            store_right(keep_right, halves(keep[...]))

        refine(flat(corner(s0, s0)), 0, f0, rx0)
        l10 = dot(flat(corner(s1, s0)), rx0[...]).astype(bf)
        store_right(rm01, corner(s0, s1))
        m11 = (flat(corner(s1, s1)).astype(f32) - dot(l10, rm01[...])).astype(bf)
        refine(m11, 1, f1, rx1)
        for tc in range(2):
            store_right(ru0, (from_row(s0, 2 * tc), from_row(s0, 2 * tc + 1)), tc * B, 2 * B)
        product = dot(l10, ru0[...])
        for tc in range(2):
            pair = []
            for r in range(2):
                old = from_row(s1, 2 * tc + r).astype(f32)
                at = (2 * r + tc) * B
                pair.append(jnp.where(cols0[tc], old - product[:, at:at + B], old).astype(bf))
            store_right(ru1, pair, tc * B, 2 * B)
        for q in range(4):
            flags = [taken((2 * q + t) * 8 + z) for t in range(2)]
            rows = [pl.ds((2 * q + t) * B, B) for t in range(2)]
            both = pl.ds(2 * q * B, 2 * B)

            def panel(s, q=q):
                return jnp.concatenate([flat([from_column(s, r, 2 * q + t) for r in range(2)]) for t in range(2)], axis=0)

            def mixed(product, old, which):
                return jnp.concatenate(
                    [
                        jnp.where(flags[t][which], product[t * B:(t + 1) * B], old[t * B:(t + 1) * B])
                        for t in range(2)
                    ],
                    axis=0,
                ).astype(bf)

            old = panel(s0)
            left = mixed(dot(old, rx0[...]), old.astype(f32), 0)
            l0[both, :] = left
            old = panel(s1).astype(f32)
            moved = mixed(old - dot(left, rm01[...]), old, 0)
            l1[both, :] = mixed(dot(moved, rx1[...]), moved.astype(f32), 1)

    first = dot(l0[pl.ds(2 * group * B, 2 * B), :], ru0[...])
    second = dot(l1[pl.ds(2 * group * B, 2 * B), :], ru1[...])
    for t in range(2):
        take0, take1 = taken((2 * group + t) * 8 + z)
        for tc in range(2):
            use0 = take0 & cols0[tc] & (col_ids[tc] != p1)
            use1 = take1 & cols1[tc]
            for r in range(2):
                old = d_ref[tc, group, 2 * r + t].astype(f32)
                at = (2 * r + tc) * B
                rows = slice(t * B, (t + 1) * B)
                old = jnp.where(use0, old - first[rows, at:at + B], old).astype(bf).astype(f32)
                tile[t, tc, r] = jnp.where(use1, old - second[rows, at:at + B], old).astype(bf)

    for tc in range(2):
        for pivot, left, factor in ((p0, l0, f0), (p1, l1, f1)):
            @pl.when(col_ids[tc] == pivot)
            def _(tc=tc, pivot=pivot, left=left, factor=factor):
                for t in range(2):
                    is_pivot = (2 * group + t) * 8 + z == pivot
                    for r in range(2):
                        lanes = pl.ds(r * B, B)
                        other = left[pl.ds((2 * group + t) * B, B), lanes].astype(f32)
                        tile[t, tc, r] = jnp.where(is_pivot, factor[:, lanes].astype(f32), other).astype(bf)

    out_row = lax.broadcasted_iota(jnp.int32, (B, B), 0)
    in_row = lax.broadcasted_iota(jnp.int32, (B, B), 1)
    perm = jnp.where(out_row == (in_row % 64) * 4 + in_row // 64, 1.0, 0.0).astype(bf)
    for t in range(2):
        for r in range(2):
            for half in range(2):
                stacked = jnp.concatenate(
                    [
                        jnp.concatenate(
                            [tile[t, tc, r, pl.ds((2 * half + s) * 64, 64), pl.ds(lb * 128, 128)] for s in range(2)],
                            axis=1,
                        )
                        for lb in range(2)
                        for tc in range(2)
                    ],
                    axis=0,
                )
                woven = dot(perm, stacked).astype(bf)
                for s in range(2):
                    o_ref[r, t, pl.ds((2 * half + s) * B, B), :] = woven[:, s * 128:(s + 1) * 128]


def update(pivots, col_lists, row_lists, inverses, x, u, k, d):
    smem = pl.BlockSpec(memory_space=pltpu.SMEM)
    vmem_in = pl.BlockSpec(memory_space=pltpu.VMEM)
    square = pltpu.VMEM((2 * B, 2 * B), jnp.bfloat16)
    flat_square = pltpu.VMEM((B, 2 * B), jnp.bfloat16)
    wide = pltpu.VMEM((2 * B, 4 * B), jnp.bfloat16)
    panel = pltpu.VMEM((8 * B, 2 * B), jnp.bfloat16)
    return pl.pallas_call(
        update_kernel,
        name="update",
        grid=(4,),
        out_shape=jax.ShapeDtypeStruct((2, 8, 4 * B, 128), jnp.bfloat16),
        in_specs=[smem] * 3 + [vmem_in] * 5,
        out_specs=pl.BlockSpec((2, 2, 4 * B, 128), lambda g: (0, g, 0, 0)),
        scratch_shapes=[
            flat_square, flat_square, square, square, square, wide, wide, square, panel, panel,
            pltpu.VMEM((2, 2, 2, B, B), jnp.bfloat16),
        ],
        compiler_params=pltpu.CompilerParams(vmem_limit_bytes=32 * 2**20),
    )(pivots, col_lists, row_lists, inverses, x, u, k, d)


def shards(matrix, inverses, pivots, col_lists, row_lists):
    packed = matrix.reshape(2, 8, B, 2, 2, 128).transpose(0, 1, 2, 4, 3, 5).reshape(2, 8, 4 * B, 128)
    d, colq, col63, rowq, row63 = split(pivots, packed)
    x, u, k = gather(pivots, colq, col63, rowq, row63)
    out = update(pivots, col_lists, row_lists, inverses, x, u, k, d)
    return out.reshape(2, 8, B, 2, 2, 128).transpose(0, 1, 2, 4, 3, 5).reshape(matrix.shape)


def solution(mesh):
    tiled = P(None, None, "row", None, None, "col", None)
    return jax.shard_map(shards, mesh=mesh, in_specs=(tiled, P(), P(), P(), P()), out_specs=tiled, check_vma=False)
```

```python
import jax
import jax.numpy as jnp
from jax import lax
from jax.experimental import pallas as pl
from jax.experimental.pallas import tpu as pltpu
from jax.sharding import PartitionSpec as P

MESH = pl.DeviceIdType.MESH
B = 256
HALF = 128
SLAB = 32


def gather_kernel(
    piv_ref, colq, col63, rowq, row63, xbuf, ubuf, kbuf,
    other_q, picked, from_chips, other_63, xown, from_rows, uown, mine_c, other_c, from_x, picked_c, from_y, kown,
    s_half, s_col, s_col63, s_ax, s_ay, s_row, s_row63, s_urow, s_cor, s_cx, s_cy, s_krow, s_xsib, s_ksib,
    r_half, r_col, r_col63, r_ax, r_ay, r_row, r_row63, r_urow, r_cor, r_cx, r_cy, r_krow, r_xsib, r_ksib,
):
    z = lax.axis_index("row")
    c = lax.axis_index("col")
    chip, core = c // 2, c % 2
    last_chip = chip == 15
    q = jnp.where(piv_ref[0] == 63, piv_ref[1], piv_ref[0])
    q_row, q_chip, q_core = q % 8, (q % 32) // 2, q % 2
    q_here = q_core == core
    cx, cy = chip % 4, chip // 4
    sibling = (z, chip * 2 + 1 - core)

    def to_chip(step):
        return lax.rem(chip + step, 16)

    def to_row(step):
        return lax.rem(z + step, 8)

    def remote(src, dst, ssem, rsem, to):
        return pltpu.make_async_remote_copy(
            src_ref=src, dst_ref=dst, send_sem=ssem, recv_sem=rsem, device_id=to, device_id_type=MESH
        )

    def on_chip(p):
        return (z, p * 2 + core)

    def on_row(w):
        return (w, c)

    def x_mate(i):
        return lax.rem(cx + i, 4)

    def y_mate(i):
        return lax.rem(cy + i, 4)

    def on_x(v):
        return on_chip(cy * 4 + v)

    def on_y(v):
        return on_chip(v * 4 + cx)

    bar = pltpu.get_barrier_semaphore()

    def greet_chip(i, carry):
        pl.semaphore_signal(bar, inc=1, device_id=on_chip(to_chip(i)), device_id_type=MESH)
        return carry

    def greet_row(i, carry):
        pl.semaphore_signal(bar, inc=1, device_id=on_row(to_row(i)), device_id_type=MESH)
        return carry

    lax.fori_loop(1, 16, greet_chip, 0)
    lax.fori_loop(1, 8, greet_row, 0)
    pl.semaphore_signal(bar, inc=1, device_id=sibling, device_id_type=MESH)
    pl.semaphore_wait(bar, 23)

    half_q = remote(colq.at[:, 1 - core], other_q, s_half.at[0], r_half.at[0], sibling)
    half_63 = remote(col63.at[:, 0], other_63, s_half.at[1], r_half.at[1], sibling)
    half_q.start()

    @pl.when(last_chip & (core == 1))
    def _():
        half_63.start()

    def send_row(i, carry):
        w = to_row(i)
        remote(rowq.at[w], from_rows.at[z], s_row.at[i], r_row.at[z], on_row(w)).start()

        @pl.when(z == 7)
        def _():
            remote(row63.at[w], uown.at[1], s_row63.at[i], r_row63.at[0], on_row(w)).start()
        return carry

    lax.fori_loop(1, 8, send_row, 0)

    @pl.when(last_chip & (core == 0))
    def _():
        half_63.wait_recv()

    @pl.when(last_chip)
    def _():
        def send_63(i, carry):
            p = to_chip(i)

            @pl.when(core == 0)
            def _():
                remote(other_63.at[p], xown.at[1], s_col63.at[i], r_col63.at[0], on_chip(p)).start()

            @pl.when(core == 1)
            def _():
                remote(col63.at[p, 1], xown.at[1], s_col63.at[i], r_col63.at[0], on_chip(p)).start()
            return carry

        lax.fori_loop(1, 16, send_63, 0)

    half_q.wait_recv()

    def pick(i, carry):
        picked[i] = jnp.where(q_here, colq[i, core], other_q[i])
        return carry

    lax.fori_loop(0, 16, pick, 0)

    def send_col(i, carry):
        p = to_chip(i)
        remote(picked.at[p], from_chips.at[chip], s_col.at[i], r_col.at[chip], on_chip(p)).start()
        return carry

    lax.fori_loop(1, 16, send_col, 0)
    from_chips[chip] = picked[chip]

    @pl.when(last_chip)
    def _():
        xown[1] = jnp.where(core == 0, other_63[15], col63[15, 1])

    from_rows[z] = rowq[z]

    @pl.when(z == 7)
    def _():
        uown[1] = row63[7]

    def wait_row(i, carry):
        w = to_row(i)
        remote(from_rows.at[w], from_rows.at[w], s_row.at[i], r_row.at[w], on_row(w)).wait_recv()
        return carry

    lax.fori_loop(1, 8, wait_row, 0)
    uown[0] = from_rows[q_row]

    @pl.when(z != 7)
    def _():
        remote(uown.at[1], uown.at[1], s_row63.at[0], r_row63.at[0], on_row(z)).wait_recv()

    q_tc = q // 32
    for a in range(2):
        for r in range(2):
            mine_c[a, 0, r] = uown[a, 2 * q_tc + r]
            mine_c[a, 1, r] = uown[a, 2 + r]
    cor = remote(mine_c.at[1 - core], other_c, s_cor.at[0], r_cor.at[0], sibling)
    cor.start()

    def line_send(line, src):
        view, ssem, rsem, me, mate, on = line
        for i in (1, 3):
            remote(src, view(me), ssem.at[i], rsem.at[me], on(mate(i))).start()

    def line_pass(line):
        view, ssem, rsem, me, mate, on = line
        for i, half in ((3, 0), (1, 1)):
            v = mate(i)
            remote(view(v), view(v), ssem.at[i], rsem.at[v], on(v)).wait_recv()
            part = view(v, half)
            remote(part, part, ssem.at[2 * half], rsem.at[4 + half], on(mate(4 - i))).start()

    def line_end(line):
        view, ssem, rsem, me, mate, on = line
        for half in range(2):
            part = view(mate(2), half)
            remote(part, part, ssem.at[2 * half], rsem.at[4 + half], on(mate(2))).wait_recv()

    def line_sent(line, src):
        view, ssem, rsem, me, mate, on = line
        for i in (1, 3):
            remote(src, src, ssem.at[i], rsem.at[0], on(mate(i))).wait_send()
        for half in range(2):
            part = view(me, half)
            remote(part, part, ssem.at[2 * half], rsem.at[0], on(mate(1))).wait_send()

    def rows_of(half):
        return pl.ds(0, HALF) if half is None else pl.ds(half * (HALF // 2), HALF // 2)

    def y_unit(v, half=None):
        return xbuf.at[1, core, v, cx, rows_of(half)]

    def x_lines(v, half=None):
        return xbuf.at[1, core, :, v, rows_of(half)]

    def x_unit(v, half=None):
        return xbuf.at[0, core, cy, v, rows_of(half)]

    def y_lines(v, half=None):
        return xbuf.at[0, core, v, :, rows_of(half)]

    line_63y = (y_unit, s_ay.at[1], r_ay.at[1], cy, y_mate, on_y)
    line_63x = (x_lines, s_ax.at[1], r_ax.at[1], cx, x_mate, on_x)
    line_qx = (x_unit, s_ax.at[0], r_ax.at[0], cx, x_mate, on_x)
    line_qy = (y_lines, s_ay.at[0], r_ay.at[0], cy, y_mate, on_y)

    def ring_send(ring, src):
        view, ssem, rsem = ring
        remote(src, view(z), ssem.at[0], rsem.at[z], on_row(to_row(1))).start()
        remote(src, view(z), ssem.at[4], rsem.at[z], on_row(to_row(7))).start()

    def ring_pass(ring, step):
        view, ssem, rsem = ring
        part = view(to_row(8 - step))
        remote(part, part, ssem.at[0], rsem.at[to_row(8 - step)], on_row(z)).wait_recv()
        if step < 4:
            remote(part, part, ssem.at[step], rsem.at[to_row(8 - step)], on_row(to_row(1))).start()
            part = view(to_row(step))
            remote(part, part, ssem.at[4], rsem.at[to_row(step)], on_row(z)).wait_recv()
        if step < 3:
            remote(part, part, ssem.at[4 + step], rsem.at[to_row(step)], on_row(to_row(7))).start()

    def ring_sent(ring):
        view, ssem, rsem = ring
        for i in range(7):
            remote(view(0), view(0), ssem.at[i], rsem.at[0], on_row(z)).wait_send()

    ring_u = (lambda w: ubuf.at[w], s_urow, r_urow)
    ring_k = (lambda w: kbuf.at[core, w], s_krow, r_krow)

    cor.wait_recv()
    for b, here in ((0, q_here), (1, core == 1)):
        from_x[cx, b] = jnp.where(here, mine_c[core, b], other_c[b])
    for i in range(1, 4):
        remote(from_x.at[cx], from_x.at[cx], s_cx.at[i], r_cx.at[cx], on_x(x_mate(i))).start()
    ring_send(ring_u, uown)
    ubuf[z] = uown[...]
    for i in range(1, 4):
        v = x_mate(i)
        remote(from_x.at[v], from_x.at[v], s_cx.at[i], r_cx.at[v], on_x(v)).wait_recv()
    picked_c[0] = from_x[q_chip % 4, 0]
    picked_c[1] = from_x[3, 1]
    for i in range(1, 4):
        remote(picked_c, from_y.at[cy], s_cy.at[i], r_cy.at[cy], on_y(y_mate(i))).start()
    from_y[cy] = picked_c[...]
    ring_pass(ring_u, 1)

    for i in range(1, 4):
        v = y_mate(i)
        remote(picked_c, from_y.at[v], s_cy.at[i], r_cy.at[v], on_y(v)).wait_recv()
    kown[0] = from_y[q_chip // 4, 0]
    kown[1] = from_y[3, 1]
    ring_send(ring_k, kown)
    kbuf[core, z] = kown[...]

    @pl.when(jnp.logical_not(last_chip))
    def _():
        remote(xown.at[1], xown.at[1], s_col63.at[0], r_col63.at[0], sibling).wait_recv()

    line_send(line_63y, xown.at[1])
    xbuf[1, core, cy, cx] = xown[1]
    ring_pass(ring_u, 2)

    def wait_col(i, carry):
        p = to_chip(i)
        remote(from_chips.at[p], from_chips.at[p], s_col.at[i], r_col.at[p], on_chip(p)).wait_recv()
        return carry

    lax.fori_loop(1, 16, wait_col, 0)
    xown[0] = from_chips[q_chip]
    line_send(line_qx, xown.at[0])
    xbuf[0, core, cy, cx] = xown[0]
    ring_pass(ring_k, 1)
    line_pass(line_63y)
    line_pass(line_qx)
    ring_pass(ring_u, 3)
    ring_pass(ring_k, 2)
    line_end(line_63y)
    line_send(line_63x, x_lines(cx))
    line_end(line_qx)
    line_send(line_qy, y_lines(cy))

    def to_sibling(part, i):
        remote(part, part, s_xsib.at[i], r_xsib.at[i], sibling).start()

    to_sibling(xbuf.at[0, core, cy], 0)
    ring_pass(ring_k, 3)
    ring_pass(ring_u, 4)
    line_pass(line_63x)
    line_pass(line_qy)
    ring_pass(ring_k, 4)
    both = remote(kbuf.at[core], kbuf.at[core], s_ksib.at[0], r_ksib.at[0], sibling)
    both.start()
    to_sibling(xbuf.at[0, core, y_mate(1)], 1)
    to_sibling(xbuf.at[0, core, y_mate(3)], 3)
    line_end(line_63x)
    to_sibling(xbuf.at[1, core], 4)
    line_end(line_qy)
    to_sibling(xbuf.at[0, core, y_mate(2)], 2)

    half_q.wait_send()
    cor.wait_send()

    @pl.when(last_chip & (core == 1))
    def _():
        half_63.wait_send()

    def sent_rows(i, carry):
        to = on_row(to_row(i))
        remote(rowq.at[0], from_rows.at[0], s_row.at[i], r_row.at[0], to).wait_send()

        @pl.when(z == 7)
        def _():
            remote(row63.at[0], uown.at[1], s_row63.at[i], r_row63.at[0], to).wait_send()
        return carry

    lax.fori_loop(1, 8, sent_rows, 0)

    def sent_chips(i, carry):
        to = on_chip(to_chip(i))
        remote(picked.at[0], from_chips.at[0], s_col.at[i], r_col.at[0], to).wait_send()

        @pl.when(last_chip)
        def _():
            remote(picked.at[0], xown.at[1], s_col63.at[i], r_col63.at[0], to).wait_send()
        return carry

    lax.fori_loop(1, 16, sent_chips, 0)
    ring_sent(ring_u)
    ring_sent(ring_k)
    line_sent(line_63y, xown.at[1])
    line_sent(line_63x, x_lines(cx))
    line_sent(line_qx, xown.at[0])
    line_sent(line_qy, y_lines(cy))
    for i in range(1, 4):
        remote(picked_c, picked_c, s_cx.at[i], r_cx.at[0], sibling).wait_send()
        remote(picked_c, picked_c, s_cy.at[i], r_cy.at[0], sibling).wait_send()
    for i in range(4):
        line = xbuf.at[0, 1 - core, y_mate(i)]
        remote(line, line, s_xsib.at[i], r_xsib.at[i], sibling).wait()
    whole = xbuf.at[1, 1 - core]
    remote(whole, whole, s_xsib.at[4], r_xsib.at[4], sibling).wait()
    both.wait_send()
    remote(kbuf.at[1 - core], kbuf.at[1 - core], s_ksib.at[0], r_ksib.at[0], sibling).wait_recv()


def gather(pivots, colq, col63, rowq, row63):
    bf = jnp.bfloat16
    shape = jax.ShapeDtypeStruct
    vmem = pl.BlockSpec(memory_space=pltpu.VMEM)
    dma = pltpu.SemaphoreType.DMA
    sems = [dma(n) for n in ((2,), (16,), (16,), (2, 6), (2, 6), (8,), (8,), (8,), (1,), (4,), (4,), (8,), (5,), (1,))]
    return pl.pallas_call(
        gather_kernel,
        name="gather_0",
        out_shape=[
            shape((2, 2, 4, 4, HALF, B), bf),
            shape((8, 2, 4, SLAB, B), bf),
            shape((2, 8, 2, 2, SLAB, B), bf),
        ],
        in_specs=[pl.BlockSpec(memory_space=pltpu.SMEM)] + [vmem] * 4,
        out_specs=[vmem] * 3,
        scratch_shapes=[
            pltpu.VMEM((16, HALF, B), bf), pltpu.VMEM((16, HALF, B), bf), pltpu.VMEM((16, HALF, B), bf),
            pltpu.VMEM((16, HALF, B), bf), pltpu.VMEM((2, HALF, B), bf),
            pltpu.VMEM((8, 4, SLAB, B), bf), pltpu.VMEM((2, 4, SLAB, B), bf),
            pltpu.VMEM((2, 2, 2, SLAB, B), bf), pltpu.VMEM((2, 2, SLAB, B), bf),
            pltpu.VMEM((4, 2, 2, SLAB, B), bf), pltpu.VMEM((2, 2, SLAB, B), bf),
            pltpu.VMEM((4, 2, 2, SLAB, B), bf), pltpu.VMEM((2, 2, SLAB, B), bf),
        ] + sems + sems,
        compiler_params=pltpu.CompilerParams(collective_id=0, has_side_effects=True, vmem_limit_bytes=24 * 2**20),
    )(pivots, colq, col63, rowq, row63)


def split_kernel(piv_ref, m_ref, d_ref, colq_ref, col63_ref, rowq_ref, row63_ref):
    group = pl.program_id(0)
    other = jnp.where(piv_ref[0] == 63, piv_ref[1], piv_ref[0])
    out_row = lax.broadcasted_iota(jnp.int32, (B, B), 0)
    in_row = lax.broadcasted_iota(jnp.int32, (B, B), 1)
    perm = jnp.where(in_row == (out_row % 64) * 4 + out_row // 64, 1.0, 0.0).astype(jnp.bfloat16)
    for r in range(2):
        for t in range(2):
            j = 2 * r + t
            for half in range(2):
                pair = jnp.concatenate([m_ref[r, t, pl.ds((2 * half + s) * B, B), :] for s in range(2)], axis=1)
                sorted_rows = jnp.dot(perm, pair, preferred_element_type=jnp.float32).astype(jnp.bfloat16)
                for s in range(2):
                    for lb in range(2):
                        for tc in range(2):
                            piece = sorted_rows[(lb * 2 + tc) * 64:(lb * 2 + tc + 1) * 64, s * 128:(s + 1) * 128]
                            here = (pl.ds((2 * half + s) * 64, 64), pl.ds(lb * 128, 128))
                            d_ref[(tc, group, j, *here)] = piece

            for h in range(2):
                rows = pl.ds(h * HALF, HALF)
                colq_ref[8 * r + 2 * group + t, h] = d_ref[other // 32, group, j, rows]
                col63_ref[8 * r + 2 * group + t, h] = d_ref[1, group, j, rows]

            @pl.when(other // 8 == 2 * group + t)
            def _(r=r, j=j):
                for tc in range(2):
                    for w in range(8):
                        rowq_ref[w, 2 * tc + r] = d_ref[tc, group, j, pl.ds(w * SLAB, SLAB)]

            if t == 1:
                @pl.when(group == 3)
                def _(r=r, j=j):
                    for tc in range(2):
                        for w in range(8):
                            row63_ref[w, 2 * tc + r] = d_ref[tc, group, j, pl.ds(w * SLAB, SLAB)]


def split(pivots, packed):
    shape = jax.ShapeDtypeStruct
    vmem = pl.BlockSpec(memory_space=pltpu.VMEM)
    return pl.pallas_call(
        split_kernel,
        name="split",
        grid=(4,),
        out_shape=[
            shape((2, 4, 4, B, B), jnp.bfloat16),
            shape((16, 2, HALF, B), jnp.bfloat16),
            shape((16, 2, HALF, B), jnp.bfloat16),
            shape((8, 4, SLAB, B), jnp.bfloat16),
            shape((8, 4, SLAB, B), jnp.bfloat16),
        ],
        in_specs=[
            pl.BlockSpec(memory_space=pltpu.SMEM),
            pl.BlockSpec((2, 2, 4 * B, 128), lambda g: (0, g, 0, 0)),
        ],
        out_specs=[vmem] * 5,
        compiler_params=pltpu.CompilerParams(vmem_limit_bytes=24 * 2**20),
    )(pivots, packed)


def dot(left, right):
    return jnp.dot(left, right, preferred_element_type=jnp.float32)


def flat(pair):
    return jnp.concatenate([pair[0], pair[1]], axis=1)


def store_right(ref, pair, at=0, width=B):
    ref[pl.ds(0, B), pl.ds(at, B)] = pair[0]
    ref[pl.ds(B, B), pl.ds(at, B)] = -pair[1]
    ref[pl.ds(0, B), pl.ds(at + width, B)] = pair[1]
    ref[pl.ds(B, B), pl.ds(at + width, B)] = pair[0]


def halves(wide):
    return wide[:, :B], wide[:, B:]


def update_kernel(
    piv_ref, cl_ref, rl_ref, inv_ref, x_ref, u_ref, k_ref, d_ref, o_ref,
    f0, f1, rx0, rx1, rm01, ru0, ru1, tmp, l0, l1, tile,
):
    bf, f32 = jnp.bfloat16, jnp.float32
    group = pl.program_id(0)
    z = lax.axis_index("row")
    c = lax.axis_index("col")
    p0, p1 = piv_ref[0], piv_ref[1]
    s0 = jnp.where(p0 == 63, 1, 0)
    s1 = 1 - s0
    col_ids = [tc * 32 + c for tc in range(2)]
    cols0 = [(rl_ref[0, i] > 0) & (i != p0) for i in col_ids]
    cols1 = [(rl_ref[1, i] > 0) & (i != p0) & (i != p1) for i in col_ids]

    def from_column(s, r, row):
        return jnp.concatenate([x_ref[s, h, 2 * r + row // 4, row % 4] for h in range(2)], axis=0)

    def from_row(s, at):
        return jnp.concatenate([u_ref[w, s, at] for w in range(8)], axis=0)

    def corner(row, col):
        return [jnp.concatenate([k_ref[row, w, col, r] for w in range(8)], axis=0) for r in range(2)]

    def taken(row):
        return (cl_ref[0, row] > 0) & (row != p0), (cl_ref[1, row] > 0) & (row != p0) & (row != p1)

    @pl.when(group == 0)
    def _():
        def refine(diagonal, step, keep, keep_right):
            guess = (inv_ref[step, 0], inv_ref[step, 1])
            store_right(tmp, guess)
            eye = lax.broadcasted_iota(jnp.int32, (B, B), 0) == lax.broadcasted_iota(jnp.int32, (B, B), 1)
            real, imag = halves(dot(diagonal, tmp[...]))
            store_right(tmp, ((jnp.where(eye, 2.0, 0.0) - real).astype(bf), (-imag).astype(bf)))
            keep[...] = dot(flat(guess), tmp[...]).astype(bf)
            store_right(keep_right, halves(keep[...]))

        refine(flat(corner(s0, s0)), 0, f0, rx0)
        l10 = dot(flat(corner(s1, s0)), rx0[...]).astype(bf)
        store_right(rm01, corner(s0, s1))
        m11 = (flat(corner(s1, s1)).astype(f32) - dot(l10, rm01[...])).astype(bf)
        refine(m11, 1, f1, rx1)
        for tc in range(2):
            store_right(ru0, (from_row(s0, 2 * tc), from_row(s0, 2 * tc + 1)), tc * B, 2 * B)
        product = dot(l10, ru0[...])
        for tc in range(2):
            pair = []
            for r in range(2):
                old = from_row(s1, 2 * tc + r).astype(f32)
                at = (2 * r + tc) * B
                pair.append(jnp.where(cols0[tc], old - product[:, at:at + B], old).astype(bf))
            store_right(ru1, pair, tc * B, 2 * B)
        for q in range(4):
            flags = [taken((2 * q + t) * 8 + z) for t in range(2)]
            rows = [pl.ds((2 * q + t) * B, B) for t in range(2)]
            both = pl.ds(2 * q * B, 2 * B)

            def panel(s, q=q):
                return jnp.concatenate([flat([from_column(s, r, 2 * q + t) for r in range(2)]) for t in range(2)], axis=0)

            def mixed(product, old, which):
                return jnp.concatenate(
                    [
                        jnp.where(flags[t][which], product[t * B:(t + 1) * B], old[t * B:(t + 1) * B])
                        for t in range(2)
                    ],
                    axis=0,
                ).astype(bf)

            old = panel(s0)
            left = mixed(dot(old, rx0[...]), old.astype(f32), 0)
            l0[both, :] = left
            old = panel(s1).astype(f32)
            moved = mixed(old - dot(left, rm01[...]), old, 0)
            l1[both, :] = mixed(dot(moved, rx1[...]), moved.astype(f32), 1)

    first = dot(l0[pl.ds(2 * group * B, 2 * B), :], ru0[...])
    second = dot(l1[pl.ds(2 * group * B, 2 * B), :], ru1[...])
    for t in range(2):
        take0, take1 = taken((2 * group + t) * 8 + z)
        for tc in range(2):
            use0 = take0 & cols0[tc] & (col_ids[tc] != p1)
            use1 = take1 & cols1[tc]
            for r in range(2):
                old = d_ref[tc, group, 2 * r + t].astype(f32)
                at = (2 * r + tc) * B
                rows = slice(t * B, (t + 1) * B)
                old = jnp.where(use0, old - first[rows, at:at + B], old).astype(bf).astype(f32)
                tile[t, tc, r] = jnp.where(use1, old - second[rows, at:at + B], old).astype(bf)

    for tc in range(2):
        for pivot, left, factor in ((p0, l0, f0), (p1, l1, f1)):
            @pl.when(col_ids[tc] == pivot)
            def _(tc=tc, pivot=pivot, left=left, factor=factor):
                for t in range(2):
                    is_pivot = (2 * group + t) * 8 + z == pivot
                    for r in range(2):
                        lanes = pl.ds(r * B, B)
                        other = left[pl.ds((2 * group + t) * B, B), lanes].astype(f32)
                        tile[t, tc, r] = jnp.where(is_pivot, factor[:, lanes].astype(f32), other).astype(bf)

    out_row = lax.broadcasted_iota(jnp.int32, (B, B), 0)
    in_row = lax.broadcasted_iota(jnp.int32, (B, B), 1)
    perm = jnp.where(out_row == (in_row % 64) * 4 + in_row // 64, 1.0, 0.0).astype(bf)
    for t in range(2):
        for r in range(2):
            for half in range(2):
                stacked = jnp.concatenate(
                    [
                        jnp.concatenate(
                            [tile[t, tc, r, pl.ds((2 * half + s) * 64, 64), pl.ds(lb * 128, 128)] for s in range(2)],
                            axis=1,
                        )
                        for lb in range(2)
                        for tc in range(2)
                    ],
                    axis=0,
                )
                woven = dot(perm, stacked).astype(bf)
                for s in range(2):
                    o_ref[r, t, pl.ds((2 * half + s) * B, B), :] = woven[:, s * 128:(s + 1) * 128]


def update(pivots, col_lists, row_lists, inverses, x, u, k, d):
    smem = pl.BlockSpec(memory_space=pltpu.SMEM)
    vmem_in = pl.BlockSpec(memory_space=pltpu.VMEM)
    square = pltpu.VMEM((2 * B, 2 * B), jnp.bfloat16)
    flat_square = pltpu.VMEM((B, 2 * B), jnp.bfloat16)
    wide = pltpu.VMEM((2 * B, 4 * B), jnp.bfloat16)
    panel = pltpu.VMEM((8 * B, 2 * B), jnp.bfloat16)
    return pl.pallas_call(
        update_kernel,
        name="update",
        grid=(4,),
        out_shape=jax.ShapeDtypeStruct((2, 8, 4 * B, 128), jnp.bfloat16),
        in_specs=[smem] * 3 + [vmem_in] * 5,
        out_specs=pl.BlockSpec((2, 2, 4 * B, 128), lambda g: (0, g, 0, 0)),
        scratch_shapes=[
            flat_square, flat_square, square, square, square, wide, wide, square, panel, panel,
            pltpu.VMEM((2, 2, 2, B, B), jnp.bfloat16),
        ],
        compiler_params=pltpu.CompilerParams(vmem_limit_bytes=32 * 2**20),
    )(pivots, col_lists, row_lists, inverses, x, u, k, d)


def shards(matrix, inverses, pivots, col_lists, row_lists):
    packed = matrix.reshape(2, 8, B, 2, 2, 128).transpose(0, 1, 2, 4, 3, 5).reshape(2, 8, 4 * B, 128)
    d, colq, col63, rowq, row63 = split(pivots, packed)
    x, u, k = gather(pivots, colq, col63, rowq, row63)
    out = update(pivots, col_lists, row_lists, inverses, x, u, k, d)
    return out.reshape(2, 8, B, 2, 2, 128).transpose(0, 1, 2, 4, 3, 5).reshape(matrix.shape)


def solution(mesh):
    tiled = P(None, None, "row", None, None, "col", None)
    return jax.shard_map(shards, mesh=mesh, in_specs=(tiled, P(), P(), P(), P()), out_specs=tiled, check_vma=False)
```

```python
import jax
import jax.numpy as jnp
from jax import lax
from jax.experimental import pallas as pl
from jax.experimental.pallas import tpu as pltpu
from jax.sharding import PartitionSpec as P

MESH = pl.DeviceIdType.MESH
B = 256
HALF = 128
SLAB = 32


def gather_kernel(
    piv_ref, colq, col63, rowq, row63, xbuf, ubuf, kbuf,
    other_q, picked, from_1, relay_1, got_1, from_2, relay_2, other_63, xown, from_rows, uown, mine_c, other_c, from_x, picked_c, from_y, kown, relay,
    s_half, s_e1, s_e2, s_col63, s_ax, s_ay, s_row, s_row63, s_urow, s_cor, s_cx, s_cy, s_krow, s_xsib, s_ksib, s_relay,
    r_half, r_e1, r_e2, r_col63, r_ax, r_ay, r_row, r_row63, r_urow, r_cor, r_cx, r_cy, r_krow, r_xsib, r_ksib, r_relay,
):
    z = lax.axis_index("row")
    c = lax.axis_index("col")
    chip, core = c // 2, c % 2
    last_chip = chip == 15
    q = jnp.where(piv_ref[0] == 63, piv_ref[1], piv_ref[0])
    q_row, q_chip, q_core = q % 8, (q % 32) // 2, q % 2
    q_here = q_core == core
    cx, cy = chip % 4, chip // 4
    sibling = (z, chip * 2 + 1 - core)

    def to_chip(step):
        return lax.rem(chip + step, 16)

    def to_row(step):
        return lax.rem(z + step, 8)

    def remote(src, dst, ssem, rsem, to):
        return pltpu.make_async_remote_copy(
            src_ref=src, dst_ref=dst, send_sem=ssem, recv_sem=rsem, device_id=to, device_id_type=MESH
        )

    def on_chip(p):
        return (z, p * 2 + core)

    def on_row(w):
        return (w, c)

    def x_mate(i):
        return lax.rem(cx + i, 4)

    def y_mate(i):
        return lax.rem(cy + i, 4)

    def on_x(v):
        return on_chip(cy * 4 + v)

    def on_y(v):
        return on_chip(v * 4 + cx)

    bar = pltpu.get_barrier_semaphore()

    def greet_chip(i, carry):
        pl.semaphore_signal(bar, inc=1, device_id=on_chip(to_chip(i)), device_id_type=MESH)
        return carry

    def greet_row(i, carry):
        pl.semaphore_signal(bar, inc=1, device_id=on_row(to_row(i)), device_id_type=MESH)
        return carry

    lax.fori_loop(1, 16, greet_chip, 0)
    lax.fori_loop(1, 8, greet_row, 0)
    pl.semaphore_signal(bar, inc=1, device_id=sibling, device_id_type=MESH)
    pl.semaphore_wait(bar, 23)

    half_q = remote(colq.at[:, 1 - core], other_q, s_half.at[0], r_half.at[0], sibling)
    half_63 = remote(col63.at[:, 0], other_63, s_half.at[1], r_half.at[1], sibling)
    half_q.start()

    @pl.when(last_chip & (core == 1))
    def _():
        half_63.start()

    def send_row(i, carry):
        w = to_row(i)
        remote(rowq.at[w], from_rows.at[z], s_row.at[i], r_row.at[z], on_row(w)).start()

        @pl.when(z == 7)
        def _():
            remote(row63.at[w], uown.at[1], s_row63.at[i], r_row63.at[0], on_row(w)).start()
        return carry

    lax.fori_loop(1, 8, send_row, 0)

    @pl.when(last_chip & (core == 0))
    def _():
        half_63.wait_recv()

    def part_63(p, dst, sem, i, rsem, to):
        @pl.when(core == 0)
        def _():
            remote(other_63.at[p], dst, sem.at[i], rsem, to).start()

        @pl.when(core == 1)
        def _():
            remote(col63.at[p, 1], dst, sem.at[i], rsem, to).start()

    @pl.when(last_chip)
    def _():
        def send_63(i, carry):
            p = to_chip(i)
            relayed = (p % 4 == 1) & (p // 4 != 3)

            @pl.when(jnp.logical_not(relayed))
            def _():
                part_63(p, xown.at[1], s_col63, i, r_col63.at[0], on_chip(p))

            @pl.when(relayed)
            def _():
                part_63(p, relay, s_col63, i, r_relay.at[0], on_chip(p + 2))
            return carry

        lax.fori_loop(1, 16, send_63, 0)

    half_q.wait_recv()

    first_x = core == 0
    a1, a2 = jnp.where(first_x, cx, cy), jnp.where(first_x, cy, cx)
    q1, q2 = jnp.where(first_x, q_chip % 4, q_chip // 4), jnp.where(first_x, q_chip // 4, q_chip % 4)

    def axis1(v):
        return on_chip(jnp.where(first_x, cy * 4 + v, v * 4 + cx))

    def axis2(v):
        return on_chip(jnp.where(first_x, v * 4 + cx, cy * 4 + v))

    def pick(i, carry):
        v, w = i // 4, i % 4
        p = jnp.where(first_x, w * 4 + v, v * 4 + w)
        picked[v, w] = jnp.where(q_here, colq[p, core], other_q[p])
        return carry

    lax.fori_loop(0, 16, pick, 0)

    def exchange_start(parts, got, relays, half, ssem, rsem, me, on):
        up, down, far = lax.rem(me + 1, 4), lax.rem(me + 3, 4), lax.rem(me + 2, 4)
        remote(parts.at[up], got.at[me], ssem.at[0], rsem.at[0], on(up)).start()
        remote(parts.at[down], got.at[me], ssem.at[1], rsem.at[1], on(down)).start()
        remote(parts.at[far, half(0)], relays.at[0], ssem.at[2], rsem.at[2], on(up)).start()
        remote(parts.at[far, half(1)], relays.at[1], ssem.at[3], rsem.at[3], on(down)).start()
        got[me] = parts[me]

    def exchange_pass(parts, got, relays, half, ssem, rsem, me, on):
        up, down = lax.rem(me + 1, 4), lax.rem(me + 3, 4)
        remote(relays.at[0], relays.at[0], ssem.at[2], rsem.at[2], on(down)).wait_recv()
        remote(relays.at[0], got.at[down, half(0)], ssem.at[4], rsem.at[4], on(up)).start()
        remote(relays.at[1], relays.at[1], ssem.at[3], rsem.at[3], on(up)).wait_recv()
        remote(relays.at[1], got.at[up, half(1)], ssem.at[5], rsem.at[5], on(down)).start()

    def exchange_end(parts, got, relays, half, ssem, rsem, me, on):
        up, down, far = lax.rem(me + 1, 4), lax.rem(me + 3, 4), lax.rem(me + 2, 4)
        remote(got.at[down], got.at[down], ssem.at[0], rsem.at[0], on(down)).wait_recv()
        remote(got.at[up], got.at[up], ssem.at[1], rsem.at[1], on(up)).wait_recv()
        remote(relays.at[0], got.at[far, half(0)], ssem.at[4], rsem.at[4], on(down)).wait_recv()
        remote(relays.at[1], got.at[far, half(1)], ssem.at[5], rsem.at[5], on(up)).wait_recv()

    def exchange_sent(parts, got, relays, half, ssem, rsem, me, on):
        for i in range(6):
            part = parts.at[0] if i < 2 else relays.at[0]
            remote(part, part, ssem.at[i], rsem.at[i], on(me)).wait_send()

    stage1 = (picked, from_1, relay_1, lambda h: pl.ds(2 * h, 2), s_e1, r_e1, a1, axis1)
    stage2 = (got_1, from_2, relay_2, lambda h: pl.ds(h * (HALF // 2), HALF // 2), s_e2, r_e2, a2, axis2)

    exchange_start(*stage1)
    relays = (cx == 3) & jnp.logical_not(last_chip)
    pass_63 = remote(relay, xown.at[1], s_relay.at[0], r_col63.at[0], on_chip(jnp.where(relays, chip - 2, chip)))

    @pl.when(relays)
    def _():
        remote(relay, relay, s_relay.at[0], r_relay.at[0], on_chip(chip)).wait_recv()
        pass_63.start()

    @pl.when(last_chip)
    def _():
        xown[1] = jnp.where(core == 0, other_63[15], col63[15, 1])

    exchange_pass(*stage1)

    from_rows[z] = rowq[z]

    @pl.when(z == 7)
    def _():
        uown[1] = row63[7]

    def wait_row(i, carry):
        w = to_row(i)
        remote(from_rows.at[w], from_rows.at[w], s_row.at[i], r_row.at[w], on_row(w)).wait_recv()
        return carry

    lax.fori_loop(1, 8, wait_row, 0)
    uown[0] = from_rows[q_row]

    @pl.when(z != 7)
    def _():
        remote(uown.at[1], uown.at[1], s_row63.at[0], r_row63.at[0], on_row(z)).wait_recv()

    q_tc = q // 32
    for a in range(2):
        for r in range(2):
            mine_c[a, 0, r] = uown[a, 2 * q_tc + r]
            mine_c[a, 1, r] = uown[a, 2 + r]
    cor = remote(mine_c.at[1 - core], other_c, s_cor.at[0], r_cor.at[0], sibling)
    cor.start()

    def line_send(line, src):
        view, ssem, rsem, me, mate, on = line
        for i in (1, 3):
            remote(src, view(me), ssem.at[i], rsem.at[me], on(mate(i))).start()

    def line_pass(line):
        view, ssem, rsem, me, mate, on = line
        for i, half in ((3, 0), (1, 1)):
            v = mate(i)
            remote(view(v), view(v), ssem.at[i], rsem.at[v], on(v)).wait_recv()
            part = view(v, half)
            remote(part, part, ssem.at[2 * half], rsem.at[4 + half], on(mate(4 - i))).start()

    def line_end(line):
        view, ssem, rsem, me, mate, on = line
        for half in range(2):
            part = view(mate(2), half)
            remote(part, part, ssem.at[2 * half], rsem.at[4 + half], on(mate(2))).wait_recv()

    def line_sent(line, src):
        view, ssem, rsem, me, mate, on = line
        for i in (1, 3):
            remote(src, src, ssem.at[i], rsem.at[0], on(mate(i))).wait_send()
        for half in range(2):
            part = view(me, half)
            remote(part, part, ssem.at[2 * half], rsem.at[0], on(mate(1))).wait_send()

    def rows_of(half):
        return pl.ds(0, HALF) if half is None else pl.ds(half * (HALF // 2), HALF // 2)

    def y_unit(v, half=None):
        return xbuf.at[1, core, v, cx, rows_of(half)]

    def x_lines(v, half=None):
        return xbuf.at[1, core, :, v, rows_of(half)]

    def x_unit(v, half=None):
        return xbuf.at[0, core, cy, v, rows_of(half)]

    def y_lines(v, half=None):
        return xbuf.at[0, core, v, :, rows_of(half)]

    line_63y = (y_unit, s_ay.at[1], r_ay.at[1], cy, y_mate, on_y)
    line_63x = (x_lines, s_ax.at[1], r_ax.at[1], cx, x_mate, on_x)
    line_qx = (x_unit, s_ax.at[0], r_ax.at[0], cx, x_mate, on_x)
    line_qy = (y_lines, s_ay.at[0], r_ay.at[0], cy, y_mate, on_y)

    def ring_send(ring, src):
        view, ssem, rsem = ring
        remote(src, view(z), ssem.at[0], rsem.at[z], on_row(to_row(1))).start()
        remote(src, view(z), ssem.at[4], rsem.at[z], on_row(to_row(7))).start()

    def ring_pass(ring, step):
        view, ssem, rsem = ring
        part = view(to_row(8 - step))
        remote(part, part, ssem.at[0], rsem.at[to_row(8 - step)], on_row(z)).wait_recv()
        if step < 4:
            remote(part, part, ssem.at[step], rsem.at[to_row(8 - step)], on_row(to_row(1))).start()
            part = view(to_row(step))
            remote(part, part, ssem.at[4], rsem.at[to_row(step)], on_row(z)).wait_recv()
        if step < 3:
            remote(part, part, ssem.at[4 + step], rsem.at[to_row(step)], on_row(to_row(7))).start()

    def ring_sent(ring):
        view, ssem, rsem = ring
        for i in range(7):
            remote(view(0), view(0), ssem.at[i], rsem.at[0], on_row(z)).wait_send()

    ring_u = (lambda w: ubuf.at[w], s_urow, r_urow)
    ring_k = (lambda w: kbuf.at[core, w], s_krow, r_krow)

    def to_sibling(part, i):
        remote(part, part, s_xsib.at[i], r_xsib.at[i], sibling).start()

    cor.wait_recv()
    for b, here in ((0, q_here), (1, core == 1)):
        from_x[cx, b] = jnp.where(here, mine_c[core, b], other_c[b])
    for i in range(1, 4):
        remote(from_x.at[cx], from_x.at[cx], s_cx.at[i], r_cx.at[cx], on_x(x_mate(i))).start()
    ring_send(ring_u, uown)
    ubuf[z] = uown[...]
    exchange_end(*stage1)
    got_1[...] = from_1[q1]
    exchange_start(*stage2)
    for i in range(1, 4):
        v = x_mate(i)
        remote(from_x.at[v], from_x.at[v], s_cx.at[i], r_cx.at[v], on_x(v)).wait_recv()
    picked_c[0] = from_x[q_chip % 4, 0]
    picked_c[1] = from_x[3, 1]
    for i in range(1, 4):
        remote(picked_c, from_y.at[cy], s_cy.at[i], r_cy.at[cy], on_y(y_mate(i))).start()
    from_y[cy] = picked_c[...]
    exchange_pass(*stage2)
    ring_pass(ring_u, 1)

    for i in range(1, 4):
        v = y_mate(i)
        remote(picked_c, from_y.at[v], s_cy.at[i], r_cy.at[v], on_y(v)).wait_recv()
    kown[0] = from_y[q_chip // 4, 0]
    kown[1] = from_y[3, 1]
    ring_send(ring_k, kown)
    kbuf[core, z] = kown[...]

    @pl.when(jnp.logical_not(last_chip))
    def _():
        remote(xown.at[1], xown.at[1], s_col63.at[0], r_col63.at[0], sibling).wait_recv()

    line_send(line_63y, xown.at[1])
    xbuf[1, core, cy, cx] = xown[1]
    ring_pass(ring_u, 2)

    exchange_end(*stage2)
    xown[0] = from_2[q2]
    line_send(line_qx, xown.at[0])
    xbuf[0, core, cy, cx] = xown[0]
    ring_pass(ring_k, 1)
    line_pass(line_63y)
    line_pass(line_qx)
    ring_pass(ring_k, 2)
    ring_pass(ring_u, 3)
    line_end(line_63y)
    line_send(line_63x, x_lines(cx))
    to_sibling(x_lines(cx), 4)
    line_end(line_qx)
    line_send(line_qy, y_lines(cy))

    to_sibling(xbuf.at[0, core, cy], 0)

    half_q.wait_send()
    cor.wait_send()

    @pl.when(last_chip & (core == 1))
    def _():
        half_63.wait_send()

    @pl.when(relays)
    def _():
        pass_63.wait_send()

    def sent_rows(i, carry):
        to = on_row(to_row(i))
        remote(rowq.at[0], from_rows.at[0], s_row.at[i], r_row.at[0], to).wait_send()

        @pl.when(z == 7)
        def _():
            remote(row63.at[0], uown.at[1], s_row63.at[i], r_row63.at[0], to).wait_send()
        return carry

    lax.fori_loop(1, 8, sent_rows, 0)

    @pl.when(last_chip)
    def _():
        def sent_chips(i, carry):
            remote(xown.at[1], xown.at[1], s_col63.at[i], r_col63.at[0], sibling).wait_send()
            return carry

        lax.fori_loop(1, 16, sent_chips, 0)

    exchange_sent(*stage1)
    exchange_sent(*stage2)
    line_sent(line_63y, xown.at[1])
    line_sent(line_qx, xown.at[0])
    for i in range(1, 4):
        remote(picked_c, picked_c, s_cx.at[i], r_cx.at[0], sibling).wait_send()
        remote(picked_c, picked_c, s_cy.at[i], r_cy.at[0], sibling).wait_send()
    ring_pass(ring_k, 3)
    line_pass(line_63x)
    to_sibling(x_lines(x_mate(1)), 5)
    to_sibling(x_lines(x_mate(3)), 7)
    line_pass(line_qy)
    ring_pass(ring_k, 4)
    both = remote(kbuf.at[core], kbuf.at[core], s_ksib.at[0], r_ksib.at[0], sibling)
    both.start()
    to_sibling(xbuf.at[0, core, y_mate(1)], 1)
    to_sibling(xbuf.at[0, core, y_mate(3)], 3)
    line_end(line_63x)
    to_sibling(x_lines(x_mate(2)), 6)
    ring_pass(ring_u, 4)
    ring_sent(ring_u)
    line_end(line_qy)
    to_sibling(xbuf.at[0, core, y_mate(2)], 2)

    ring_sent(ring_k)
    line_sent(line_63x, x_lines(cx))
    line_sent(line_qy, y_lines(cy))
    for i in range(4):
        line = xbuf.at[0, 1 - core, y_mate(i)]
        remote(line, line, s_xsib.at[i], r_xsib.at[i], sibling).wait()
        line = xbuf.at[1, 1 - core, :, x_mate(i)]
        remote(line, line, s_xsib.at[4 + i], r_xsib.at[4 + i], sibling).wait()
    both.wait_send()
    remote(kbuf.at[1 - core], kbuf.at[1 - core], s_ksib.at[0], r_ksib.at[0], sibling).wait_recv()


def gather(pivots, colq, col63, rowq, row63):
    bf = jnp.bfloat16
    shape = jax.ShapeDtypeStruct
    vmem = pl.BlockSpec(memory_space=pltpu.VMEM)
    dma = pltpu.SemaphoreType.DMA
    sems = [dma(n) for n in ((2,), (6,), (6,), (16,), (2, 6), (2, 6), (8,), (8,), (8,), (1,), (4,), (4,), (8,), (8,), (1,), (1,))]
    return pl.pallas_call(
        gather_kernel,
        name="gather_0",
        out_shape=[
            shape((2, 2, 4, 4, HALF, B), bf),
            shape((8, 2, 4, SLAB, B), bf),
            shape((2, 8, 2, 2, SLAB, B), bf),
        ],
        in_specs=[pl.BlockSpec(memory_space=pltpu.SMEM)] + [vmem] * 4,
        out_specs=[vmem] * 3,
        scratch_shapes=[
            pltpu.VMEM((16, HALF, B), bf), pltpu.VMEM((4, 4, HALF, B), bf), pltpu.VMEM((4, 4, HALF, B), bf),
            pltpu.VMEM((2, 2, HALF, B), bf), pltpu.VMEM((4, HALF, B), bf), pltpu.VMEM((4, HALF, B), bf),
            pltpu.VMEM((2, HALF // 2, B), bf), pltpu.VMEM((16, HALF, B), bf), pltpu.VMEM((2, HALF, B), bf),
            pltpu.VMEM((8, 4, SLAB, B), bf), pltpu.VMEM((2, 4, SLAB, B), bf),
            pltpu.VMEM((2, 2, 2, SLAB, B), bf), pltpu.VMEM((2, 2, SLAB, B), bf),
            pltpu.VMEM((4, 2, 2, SLAB, B), bf), pltpu.VMEM((2, 2, SLAB, B), bf),
            pltpu.VMEM((4, 2, 2, SLAB, B), bf), pltpu.VMEM((2, 2, SLAB, B), bf), pltpu.VMEM((HALF, B), bf),
        ] + sems + sems,
        compiler_params=pltpu.CompilerParams(collective_id=0, has_side_effects=True, vmem_limit_bytes=24 * 2**20),
    )(pivots, colq, col63, rowq, row63)


def split_kernel(piv_ref, m_ref, d_ref, colq_ref, col63_ref, rowq_ref, row63_ref):
    group = pl.program_id(0)
    other = jnp.where(piv_ref[0] == 63, piv_ref[1], piv_ref[0])
    out_row = lax.broadcasted_iota(jnp.int32, (B, B), 0)
    in_row = lax.broadcasted_iota(jnp.int32, (B, B), 1)
    perm = jnp.where(in_row == (out_row % 64) * 4 + out_row // 64, 1.0, 0.0).astype(jnp.bfloat16)
    for r in range(2):
        for t in range(2):
            j = 2 * r + t
            for half in range(2):
                pair = jnp.concatenate([m_ref[r, t, pl.ds((2 * half + s) * B, B), :] for s in range(2)], axis=1)
                sorted_rows = jnp.dot(perm, pair, preferred_element_type=jnp.float32).astype(jnp.bfloat16)
                for s in range(2):
                    for lb in range(2):
                        for tc in range(2):
                            piece = sorted_rows[(lb * 2 + tc) * 64:(lb * 2 + tc + 1) * 64, s * 128:(s + 1) * 128]
                            here = (pl.ds((2 * half + s) * 64, 64), pl.ds(lb * 128, 128))
                            d_ref[(tc, group, j, *here)] = piece

            for h in range(2):
                rows = pl.ds(h * HALF, HALF)
                colq_ref[8 * r + 2 * group + t, h] = d_ref[other // 32, group, j, rows]
                col63_ref[8 * r + 2 * group + t, h] = d_ref[1, group, j, rows]

            @pl.when(other // 8 == 2 * group + t)
            def _(r=r, j=j):
                for tc in range(2):
                    for w in range(8):
                        rowq_ref[w, 2 * tc + r] = d_ref[tc, group, j, pl.ds(w * SLAB, SLAB)]

            if t == 1:
                @pl.when(group == 3)
                def _(r=r, j=j):
                    for tc in range(2):
                        for w in range(8):
                            row63_ref[w, 2 * tc + r] = d_ref[tc, group, j, pl.ds(w * SLAB, SLAB)]


def split(pivots, packed):
    shape = jax.ShapeDtypeStruct
    vmem = pl.BlockSpec(memory_space=pltpu.VMEM)
    return pl.pallas_call(
        split_kernel,
        name="split",
        grid=(4,),
        out_shape=[
            shape((2, 4, 4, B, B), jnp.bfloat16),
            shape((16, 2, HALF, B), jnp.bfloat16),
            shape((16, 2, HALF, B), jnp.bfloat16),
            shape((8, 4, SLAB, B), jnp.bfloat16),
            shape((8, 4, SLAB, B), jnp.bfloat16),
        ],
        in_specs=[
            pl.BlockSpec(memory_space=pltpu.SMEM),
            pl.BlockSpec((2, 2, 4 * B, 128), lambda g: (0, g, 0, 0)),
        ],
        out_specs=[vmem] * 5,
        compiler_params=pltpu.CompilerParams(vmem_limit_bytes=24 * 2**20),
    )(pivots, packed)


def dot(left, right):
    return jnp.dot(left, right, preferred_element_type=jnp.float32)


def flat(pair):
    return jnp.concatenate([pair[0], pair[1]], axis=1)


def store_right(ref, pair, at=0, width=B):
    ref[pl.ds(0, B), pl.ds(at, B)] = pair[0]
    ref[pl.ds(B, B), pl.ds(at, B)] = -pair[1]
    ref[pl.ds(0, B), pl.ds(at + width, B)] = pair[1]
    ref[pl.ds(B, B), pl.ds(at + width, B)] = pair[0]


def halves(wide):
    return wide[:, :B], wide[:, B:]


def update_kernel(
    piv_ref, cl_ref, rl_ref, inv_ref, x_ref, u_ref, k_ref, d_ref, o_ref,
    f0, f1, rx0, rx1, rm01, ru0, ru1, tmp, l0, l1, tile,
):
    bf, f32 = jnp.bfloat16, jnp.float32
    group = pl.program_id(0)
    z = lax.axis_index("row")
    c = lax.axis_index("col")
    p0, p1 = piv_ref[0], piv_ref[1]
    s0 = jnp.where(p0 == 63, 1, 0)
    s1 = 1 - s0
    col_ids = [tc * 32 + c for tc in range(2)]
    cols0 = [(rl_ref[0, i] > 0) & (i != p0) for i in col_ids]
    cols1 = [(rl_ref[1, i] > 0) & (i != p0) & (i != p1) for i in col_ids]

    def from_column(s, r, row):
        return jnp.concatenate([x_ref[s, h, 2 * r + row // 4, row % 4] for h in range(2)], axis=0)

    def from_row(s, at):
        return jnp.concatenate([u_ref[w, s, at] for w in range(8)], axis=0)

    def corner(row, col):
        return [jnp.concatenate([k_ref[row, w, col, r] for w in range(8)], axis=0) for r in range(2)]

    def taken(row):
        return (cl_ref[0, row] > 0) & (row != p0), (cl_ref[1, row] > 0) & (row != p0) & (row != p1)

    @pl.when(group == 0)
    def _():
        def refine(diagonal, step, keep, keep_right, *meanwhile):
            guess = (inv_ref[step, 0], inv_ref[step, 1])
            store_right(tmp, guess)
            eye = lax.broadcasted_iota(jnp.int32, (B, B), 0) == lax.broadcasted_iota(jnp.int32, (B, B), 1)
            real, imag = halves(dot(diagonal, tmp[...]))
            if meanwhile:
                meanwhile[0]()
            store_right(tmp, ((jnp.where(eye, 2.0, 0.0) - real).astype(bf), (-imag).astype(bf)))
            keep[...] = dot(flat(guess), tmp[...]).astype(bf)
            if meanwhile:
                meanwhile[1]()
            store_right(keep_right, halves(keep[...]))

        def panel(s, q):
            return jnp.concatenate(
                [flat([from_column(s, r, 2 * q + t) for r in range(2)]) for t in range(2)], axis=0
            )

        def mixed(q, product, old, which):
            return jnp.concatenate(
                [
                    jnp.where(taken((2 * q + t) * 8 + z)[which], product[t * B:(t + 1) * B], old[t * B:(t + 1) * B])
                    for t in range(2)
                ],
                axis=0,
            ).astype(bf)

        def both(q):
            return pl.ds(2 * q * B, 2 * B)

        def first_panel(q):
            old = panel(s0, q)
            l0[both(q), :] = mixed(q, dot(old, rx0[...]), old.astype(f32), 0)

        def moved_panel(q):
            old = panel(s1, q).astype(f32)
            l1[both(q), :] = mixed(q, old - dot(l0[both(q), :], rm01[...]), old, 0)

        def second_panel(q):
            moved = l1[both(q), :]
            l1[both(q), :] = mixed(q, dot(moved, rx1[...]), moved.astype(f32), 1)

        store_right(rm01, corner(s0, s1))
        refine(flat(corner(s0, s0)), 0, f0, rx0)
        l10 = dot(flat(corner(s1, s0)), rx0[...]).astype(bf)
        first_panel(0)
        m11 = (flat(corner(s1, s1)).astype(f32) - dot(l10, rm01[...])).astype(bf)
        first_panel(1)
        refine(m11, 1, f1, rx1, lambda: (first_panel(2), first_panel(3)), lambda: (moved_panel(0), moved_panel(1)))
        for tc in range(2):
            store_right(ru0, (from_row(s0, 2 * tc), from_row(s0, 2 * tc + 1)), tc * B, 2 * B)
        product = dot(l10, ru0[...])
        for tc in range(2):
            pair = []
            for r in range(2):
                old = from_row(s1, 2 * tc + r).astype(f32)
                at = (2 * r + tc) * B
                pair.append(jnp.where(cols0[tc], old - product[:, at:at + B], old).astype(bf))
            store_right(ru1, pair, tc * B, 2 * B)

        moved_panel(2)
        moved_panel(3)
        for q in range(4):
            second_panel(q)

    first = dot(l0[pl.ds(2 * group * B, 2 * B), :], ru0[...])
    second = dot(l1[pl.ds(2 * group * B, 2 * B), :], ru1[...])
    for t in range(2):
        take0, take1 = taken((2 * group + t) * 8 + z)
        for tc in range(2):
            use0 = take0 & cols0[tc] & (col_ids[tc] != p1)
            use1 = take1 & cols1[tc]
            for r in range(2):
                old = d_ref[tc, group, 2 * r + t].astype(f32)
                at = (2 * r + tc) * B
                rows = slice(t * B, (t + 1) * B)
                old = jnp.where(use0, old - first[rows, at:at + B], old).astype(bf).astype(f32)
                tile[t, tc, r] = jnp.where(use1, old - second[rows, at:at + B], old).astype(bf)

    for tc in range(2):
        for pivot, left, factor in ((p0, l0, f0), (p1, l1, f1)):
            @pl.when(col_ids[tc] == pivot)
            def _(tc=tc, pivot=pivot, left=left, factor=factor):
                for t in range(2):
                    is_pivot = (2 * group + t) * 8 + z == pivot
                    for r in range(2):
                        lanes = pl.ds(r * B, B)
                        other = left[pl.ds((2 * group + t) * B, B), lanes].astype(f32)
                        tile[t, tc, r] = jnp.where(is_pivot, factor[:, lanes].astype(f32), other).astype(bf)

    out_row = lax.broadcasted_iota(jnp.int32, (B, B), 0)
    in_row = lax.broadcasted_iota(jnp.int32, (B, B), 1)
    perm = jnp.where(out_row == (in_row % 64) * 4 + in_row // 64, 1.0, 0.0).astype(bf)
    for t in range(2):
        for r in range(2):
            for half in range(2):
                stacked = jnp.concatenate(
                    [
                        jnp.concatenate(
                            [tile[t, tc, r, pl.ds((2 * half + s) * 64, 64), pl.ds(lb * 128, 128)] for s in range(2)],
                            axis=1,
                        )
                        for lb in range(2)
                        for tc in range(2)
                    ],
                    axis=0,
                )
                woven = dot(perm, stacked).astype(bf)
                for s in range(2):
                    o_ref[r, t, pl.ds((2 * half + s) * B, B), :] = woven[:, s * 128:(s + 1) * 128]


def update(pivots, col_lists, row_lists, inverses, x, u, k, d):
    smem = pl.BlockSpec(memory_space=pltpu.SMEM)
    vmem_in = pl.BlockSpec(memory_space=pltpu.VMEM)
    square = pltpu.VMEM((2 * B, 2 * B), jnp.bfloat16)
    flat_square = pltpu.VMEM((B, 2 * B), jnp.bfloat16)
    wide = pltpu.VMEM((2 * B, 4 * B), jnp.bfloat16)
    panel = pltpu.VMEM((8 * B, 2 * B), jnp.bfloat16)
    return pl.pallas_call(
        update_kernel,
        name="update",
        grid=(4,),
        out_shape=jax.ShapeDtypeStruct((2, 8, 4 * B, 128), jnp.bfloat16),
        in_specs=[smem] * 3 + [vmem_in] * 5,
        out_specs=pl.BlockSpec((2, 2, 4 * B, 128), lambda g: (0, g, 0, 0)),
        scratch_shapes=[
            flat_square, flat_square, square, square, square, wide, wide, square, panel, panel,
            pltpu.VMEM((2, 2, 2, B, B), jnp.bfloat16),
        ],
        compiler_params=pltpu.CompilerParams(vmem_limit_bytes=32 * 2**20),
    )(pivots, col_lists, row_lists, inverses, x, u, k, d)


def shards(matrix, inverses, pivots, col_lists, row_lists):
    packed = matrix.reshape(2, 8, B, 2, 2, 128).transpose(0, 1, 2, 4, 3, 5).reshape(2, 8, 4 * B, 128)
    d, colq, col63, rowq, row63 = split(pivots, packed)
    x, u, k = gather(pivots, colq, col63, rowq, row63)
    out = update(pivots, col_lists, row_lists, inverses, x, u, k, d)
    return out.reshape(2, 8, B, 2, 2, 128).transpose(0, 1, 2, 4, 3, 5).reshape(matrix.shape)


def solution(mesh):
    tiled = P(None, None, "row", None, None, "col", None)
    return jax.shard_map(shards, mesh=mesh, in_specs=(tiled, P(), P(), P(), P()), out_specs=tiled, check_vma=False)
```

```python
import jax
import jax.numpy as jnp
from jax import lax
from jax.experimental import pallas as pl
from jax.experimental.pallas import tpu as pltpu
from jax.sharding import PartitionSpec as P

MESH = pl.DeviceIdType.MESH
B = 256
HALF = 128
SLAB = 32


def gather_kernel(
    piv_ref, colq, col63, rowq, row63, xbuf, ubuf, kbuf,
    other_q, picked, from_1, relay_1, got_1, from_2, relay_2, other_63, xown, from_rows, uown, mine_c, other_c, from_x, picked_c, from_y, kown, relay,
    s_half, s_e1, s_e2, s_col63, s_ax, s_ay, s_row, s_row63, s_urow, s_cor, s_cx, s_cy, s_krow, s_xsib, s_ksib, s_relay,
    r_half, r_e1, r_e2, r_col63, r_ax, r_ay, r_row, r_row63, r_urow, r_cor, r_cx, r_cy, r_krow, r_xsib, r_ksib, r_relay,
):
    z = lax.axis_index("row")
    c = lax.axis_index("col")
    chip, core = c // 2, c % 2
    last_chip = chip == 15
    q = jnp.where(piv_ref[0] == 63, piv_ref[1], piv_ref[0])
    q_row, q_chip, q_core = q % 8, (q % 32) // 2, q % 2
    q_here = q_core == core
    cx, cy = chip % 4, chip // 4
    sibling = (z, chip * 2 + 1 - core)

    def to_chip(step):
        return lax.rem(chip + step, 16)

    def to_row(step):
        return lax.rem(z + step, 8)

    def remote(src, dst, ssem, rsem, to):
        return pltpu.make_async_remote_copy(
            src_ref=src, dst_ref=dst, send_sem=ssem, recv_sem=rsem, device_id=to, device_id_type=MESH
        )

    def on_chip(p):
        return (z, p * 2 + core)

    def on_row(w):
        return (w, c)

    def x_mate(i):
        return lax.rem(cx + i, 4)

    def y_mate(i):
        return lax.rem(cy + i, 4)

    def on_x(v):
        return on_chip(cy * 4 + v)

    def on_y(v):
        return on_chip(v * 4 + cx)

    bar = pltpu.get_barrier_semaphore()

    def greet_chip(i, carry):
        pl.semaphore_signal(bar, inc=1, device_id=on_chip(to_chip(i)), device_id_type=MESH)
        return carry

    def greet_row(i, carry):
        pl.semaphore_signal(bar, inc=1, device_id=on_row(to_row(i)), device_id_type=MESH)
        return carry

    lax.fori_loop(1, 16, greet_chip, 0)
    lax.fori_loop(1, 8, greet_row, 0)
    pl.semaphore_signal(bar, inc=1, device_id=sibling, device_id_type=MESH)
    pl.semaphore_wait(bar, 23)

    half_q = remote(colq.at[:, 1 - core], other_q, s_half.at[0], r_half.at[0], sibling)
    half_63 = remote(col63.at[:, 0], other_63, s_half.at[1], r_half.at[1], sibling)
    half_q.start()

    @pl.when(last_chip & (core == 1))
    def _():
        half_63.start()

    def send_row(i, carry):
        w = to_row(i)
        remote(rowq.at[w], from_rows.at[z], s_row.at[i], r_row.at[z], on_row(w)).start()

        @pl.when(z == 7)
        def _():
            remote(row63.at[w], uown.at[1], s_row63.at[i], r_row63.at[0], on_row(w)).start()
        return carry

    lax.fori_loop(1, 8, send_row, 0)

    @pl.when(last_chip & (core == 0))
    def _():
        half_63.wait_recv()

    def part_63(p, dst, sem, i, rsem, to):
        @pl.when(core == 0)
        def _():
            remote(other_63.at[p], dst, sem.at[i], rsem, to).start()

        @pl.when(core == 1)
        def _():
            remote(col63.at[p, 1], dst, sem.at[i], rsem, to).start()

    @pl.when(last_chip)
    def _():
        def send_63(i, carry):
            p = to_chip(i)
            relayed = (p % 4 == 1) & (p // 4 != 3)

            @pl.when(jnp.logical_not(relayed))
            def _():
                part_63(p, xown.at[1], s_col63, i, r_col63.at[0], on_chip(p))

            @pl.when(relayed)
            def _():
                part_63(p, relay, s_col63, i, r_relay.at[0], on_chip(p + 2))
            return carry

        lax.fori_loop(1, 16, send_63, 0)

    half_q.wait_recv()

    first_x = core == 0
    a1, a2 = jnp.where(first_x, cx, cy), jnp.where(first_x, cy, cx)
    q1, q2 = jnp.where(first_x, q_chip % 4, q_chip // 4), jnp.where(first_x, q_chip // 4, q_chip % 4)

    def axis1(v):
        return on_chip(jnp.where(first_x, cy * 4 + v, v * 4 + cx))

    def axis2(v):
        return on_chip(jnp.where(first_x, v * 4 + cx, cy * 4 + v))

    def pick(i, carry):
        v, w = i // 4, i % 4
        p = jnp.where(first_x, w * 4 + v, v * 4 + w)
        picked[v, w] = jnp.where(q_here, colq[p, core], other_q[p])
        return carry

    lax.fori_loop(0, 16, pick, 0)

    def exchange_start(parts, got, relays, half, ssem, rsem, me, on):
        up, down, far = lax.rem(me + 1, 4), lax.rem(me + 3, 4), lax.rem(me + 2, 4)
        remote(parts.at[up], got.at[me], ssem.at[0], rsem.at[0], on(up)).start()
        remote(parts.at[down], got.at[me], ssem.at[1], rsem.at[1], on(down)).start()
        remote(parts.at[far, half(0)], relays.at[0], ssem.at[2], rsem.at[2], on(up)).start()
        remote(parts.at[far, half(1)], relays.at[1], ssem.at[3], rsem.at[3], on(down)).start()
        got[me] = parts[me]

    def exchange_pass(parts, got, relays, half, ssem, rsem, me, on):
        up, down = lax.rem(me + 1, 4), lax.rem(me + 3, 4)
        remote(relays.at[0], relays.at[0], ssem.at[2], rsem.at[2], on(down)).wait_recv()
        remote(relays.at[0], got.at[down, half(0)], ssem.at[4], rsem.at[4], on(up)).start()
        remote(relays.at[1], relays.at[1], ssem.at[3], rsem.at[3], on(up)).wait_recv()
        remote(relays.at[1], got.at[up, half(1)], ssem.at[5], rsem.at[5], on(down)).start()

    def exchange_end(parts, got, relays, half, ssem, rsem, me, on):
        up, down, far = lax.rem(me + 1, 4), lax.rem(me + 3, 4), lax.rem(me + 2, 4)
        remote(got.at[down], got.at[down], ssem.at[0], rsem.at[0], on(down)).wait_recv()
        remote(got.at[up], got.at[up], ssem.at[1], rsem.at[1], on(up)).wait_recv()
        remote(relays.at[0], got.at[far, half(0)], ssem.at[4], rsem.at[4], on(down)).wait_recv()
        remote(relays.at[1], got.at[far, half(1)], ssem.at[5], rsem.at[5], on(up)).wait_recv()

    def exchange_sent(parts, got, relays, half, ssem, rsem, me, on):
        for i in range(6):
            part = parts.at[0] if i < 2 else relays.at[0]
            remote(part, part, ssem.at[i], rsem.at[i], on(me)).wait_send()

    stage1 = (picked, from_1, relay_1, lambda h: pl.ds(2 * h, 2), s_e1, r_e1, a1, axis1)
    stage2 = (got_1, from_2, relay_2, lambda h: pl.ds(h * (HALF // 2), HALF // 2), s_e2, r_e2, a2, axis2)

    exchange_start(*stage1)
    relays = (cx == 3) & jnp.logical_not(last_chip)
    pass_63 = remote(relay, xown.at[1], s_relay.at[0], r_col63.at[0], on_chip(jnp.where(relays, chip - 2, chip)))

    @pl.when(relays)
    def _():
        remote(relay, relay, s_relay.at[0], r_relay.at[0], on_chip(chip)).wait_recv()
        pass_63.start()

    @pl.when(last_chip)
    def _():
        xown[1] = jnp.where(core == 0, other_63[15], col63[15, 1])

    exchange_pass(*stage1)

    from_rows[z] = rowq[z]

    @pl.when(z == 7)
    def _():
        uown[1] = row63[7]

    def wait_row(i, carry):
        w = to_row(i)
        remote(from_rows.at[w], from_rows.at[w], s_row.at[i], r_row.at[w], on_row(w)).wait_recv()
        return carry

    lax.fori_loop(1, 8, wait_row, 0)
    uown[0] = from_rows[q_row]

    @pl.when(z != 7)
    def _():
        remote(uown.at[1], uown.at[1], s_row63.at[0], r_row63.at[0], on_row(z)).wait_recv()

    q_tc = q // 32
    for a in range(2):
        for r in range(2):
            mine_c[a, 0, r] = uown[a, 2 * q_tc + r]
            mine_c[a, 1, r] = uown[a, 2 + r]
    cor = remote(mine_c.at[1 - core], other_c, s_cor.at[0], r_cor.at[0], sibling)
    cor.start()

    def line_send(line, src):
        view, ssem, rsem, me, mate, on = line
        for i in (1, 3):
            remote(src, view(me), ssem.at[i], rsem.at[me], on(mate(i))).start()

    def line_pass(line):
        view, ssem, rsem, me, mate, on = line
        for i, half in ((3, 0), (1, 1)):
            v = mate(i)
            remote(view(v), view(v), ssem.at[i], rsem.at[v], on(v)).wait_recv()
            part = view(v, half)
            remote(part, part, ssem.at[2 * half], rsem.at[4 + half], on(mate(4 - i))).start()

    def line_end(line):
        view, ssem, rsem, me, mate, on = line
        for half in range(2):
            part = view(mate(2), half)
            remote(part, part, ssem.at[2 * half], rsem.at[4 + half], on(mate(2))).wait_recv()

    def line_sent(line, src):
        view, ssem, rsem, me, mate, on = line
        for i in (1, 3):
            remote(src, src, ssem.at[i], rsem.at[0], on(mate(i))).wait_send()
        for half in range(2):
            part = view(me, half)
            remote(part, part, ssem.at[2 * half], rsem.at[0], on(mate(1))).wait_send()

    def rows_of(half):
        return pl.ds(0, HALF) if half is None else pl.ds(half * (HALF // 2), HALF // 2)

    def y_unit(v, half=None):
        return xbuf.at[1, core, v, cx, rows_of(half)]

    def x_lines(v, half=None):
        return xbuf.at[1, core, :, v, rows_of(half)]

    def x_unit(v, half=None):
        return xbuf.at[0, core, cy, v, rows_of(half)]

    def y_lines(v, half=None):
        return xbuf.at[0, core, v, :, rows_of(half)]

    line_63y = (y_unit, s_ay.at[1], r_ay.at[1], cy, y_mate, on_y)
    line_63x = (x_lines, s_ax.at[1], r_ax.at[1], cx, x_mate, on_x)
    line_qx = (x_unit, s_ax.at[0], r_ax.at[0], cx, x_mate, on_x)
    line_qy = (y_lines, s_ay.at[0], r_ay.at[0], cy, y_mate, on_y)

    def ring_send(ring, src):
        view, ssem, rsem = ring
        remote(src, view(z), ssem.at[0], rsem.at[z], on_row(to_row(1))).start()
        remote(src, view(z), ssem.at[4], rsem.at[z], on_row(to_row(7))).start()

    def ring_pass(ring, step):
        view, ssem, rsem = ring
        part = view(to_row(8 - step))
        remote(part, part, ssem.at[0], rsem.at[to_row(8 - step)], on_row(z)).wait_recv()
        if step < 4:
            remote(part, part, ssem.at[step], rsem.at[to_row(8 - step)], on_row(to_row(1))).start()
            part = view(to_row(step))
            remote(part, part, ssem.at[4], rsem.at[to_row(step)], on_row(z)).wait_recv()
        if step < 3:
            remote(part, part, ssem.at[4 + step], rsem.at[to_row(step)], on_row(to_row(7))).start()

    def ring_sent(ring):
        view, ssem, rsem = ring
        for i in range(7):
            remote(view(0), view(0), ssem.at[i], rsem.at[0], on_row(z)).wait_send()

    ring_u = (lambda w: ubuf.at[w], s_urow, r_urow)
    ring_k = (lambda w: kbuf.at[core, w], s_krow, r_krow)

    def to_sibling(part, i):
        remote(part, part, s_xsib.at[i], r_xsib.at[i], sibling).start()

    cor.wait_recv()
    for b, here in ((0, q_here), (1, core == 1)):
        from_x[cx, b] = jnp.where(here, mine_c[core, b], other_c[b])
    for i in range(1, 4):
        remote(from_x.at[cx], from_x.at[cx], s_cx.at[i], r_cx.at[cx], on_x(x_mate(i))).start()
    ring_send(ring_u, uown)
    ubuf[z] = uown[...]
    exchange_end(*stage1)
    got_1[...] = from_1[q1]
    exchange_start(*stage2)
    for i in range(1, 4):
        v = x_mate(i)
        remote(from_x.at[v], from_x.at[v], s_cx.at[i], r_cx.at[v], on_x(v)).wait_recv()
    picked_c[0] = from_x[q_chip % 4, 0]
    picked_c[1] = from_x[3, 1]
    for i in range(1, 4):
        remote(picked_c, from_y.at[cy], s_cy.at[i], r_cy.at[cy], on_y(y_mate(i))).start()
    from_y[cy] = picked_c[...]
    exchange_pass(*stage2)
    ring_pass(ring_u, 1)

    for i in range(1, 4):
        v = y_mate(i)
        remote(picked_c, from_y.at[v], s_cy.at[i], r_cy.at[v], on_y(v)).wait_recv()
    kown[0] = from_y[q_chip // 4, 0]
    kown[1] = from_y[3, 1]
    ring_send(ring_k, kown)
    kbuf[core, z] = kown[...]

    @pl.when(jnp.logical_not(last_chip))
    def _():
        remote(xown.at[1], xown.at[1], s_col63.at[0], r_col63.at[0], sibling).wait_recv()

    line_send(line_63y, xown.at[1])
    xbuf[1, core, cy, cx] = xown[1]
    ring_pass(ring_u, 2)

    exchange_end(*stage2)
    xown[0] = from_2[q2]
    line_send(line_qx, xown.at[0])
    xbuf[0, core, cy, cx] = xown[0]
    ring_pass(ring_k, 1)
    line_pass(line_63y)
    line_pass(line_qx)
    ring_pass(ring_k, 2)
    ring_pass(ring_u, 3)
    line_end(line_63y)
    line_send(line_63x, x_lines(cx))
    to_sibling(x_lines(cx), 4)
    line_end(line_qx)
    line_send(line_qy, y_lines(cy))

    to_sibling(xbuf.at[0, core, cy], 0)

    half_q.wait_send()
    cor.wait_send()

    @pl.when(last_chip & (core == 1))
    def _():
        half_63.wait_send()

    @pl.when(relays)
    def _():
        pass_63.wait_send()

    def sent_rows(i, carry):
        to = on_row(to_row(i))
        remote(rowq.at[0], from_rows.at[0], s_row.at[i], r_row.at[0], to).wait_send()

        @pl.when(z == 7)
        def _():
            remote(row63.at[0], uown.at[1], s_row63.at[i], r_row63.at[0], to).wait_send()
        return carry

    lax.fori_loop(1, 8, sent_rows, 0)

    @pl.when(last_chip)
    def _():
        def sent_chips(i, carry):
            remote(xown.at[1], xown.at[1], s_col63.at[i], r_col63.at[0], sibling).wait_send()
            return carry

        lax.fori_loop(1, 16, sent_chips, 0)

    exchange_sent(*stage1)
    exchange_sent(*stage2)
    line_sent(line_63y, xown.at[1])
    line_sent(line_qx, xown.at[0])
    for i in range(1, 4):
        remote(picked_c, picked_c, s_cx.at[i], r_cx.at[0], sibling).wait_send()
        remote(picked_c, picked_c, s_cy.at[i], r_cy.at[0], sibling).wait_send()
    ring_pass(ring_k, 3)
    line_pass(line_63x)
    to_sibling(x_lines(x_mate(1)), 5)
    to_sibling(x_lines(x_mate(3)), 7)
    line_pass(line_qy)
    ring_pass(ring_k, 4)
    both = remote(kbuf.at[core], kbuf.at[core], s_ksib.at[0], r_ksib.at[0], sibling)
    both.start()
    to_sibling(xbuf.at[0, core, y_mate(1)], 1)
    to_sibling(xbuf.at[0, core, y_mate(3)], 3)
    line_end(line_63x)
    to_sibling(x_lines(x_mate(2)), 6)
    ring_pass(ring_u, 4)
    ring_sent(ring_u)
    line_end(line_qy)
    to_sibling(xbuf.at[0, core, y_mate(2)], 2)

    ring_sent(ring_k)
    line_sent(line_63x, x_lines(cx))
    line_sent(line_qy, y_lines(cy))
    for i in range(4):
        line = xbuf.at[0, 1 - core, y_mate(i)]
        remote(line, line, s_xsib.at[i], r_xsib.at[i], sibling).wait()
        line = xbuf.at[1, 1 - core, :, x_mate(i)]
        remote(line, line, s_xsib.at[4 + i], r_xsib.at[4 + i], sibling).wait()
    both.wait_send()
    remote(kbuf.at[1 - core], kbuf.at[1 - core], s_ksib.at[0], r_ksib.at[0], sibling).wait_recv()


def gather(pivots, colq, col63, rowq, row63):
    bf = jnp.bfloat16
    shape = jax.ShapeDtypeStruct
    vmem = pl.BlockSpec(memory_space=pltpu.VMEM)
    dma = pltpu.SemaphoreType.DMA
    sems = [dma(n) for n in ((2,), (6,), (6,), (16,), (2, 6), (2, 6), (8,), (8,), (8,), (1,), (4,), (4,), (8,), (8,), (1,), (1,))]
    return pl.pallas_call(
        gather_kernel,
        name="gather_0",
        out_shape=[
            shape((2, 2, 4, 4, HALF, B), bf),
            shape((8, 2, 4, SLAB, B), bf),
            shape((2, 8, 2, 2, SLAB, B), bf),
        ],
        in_specs=[pl.BlockSpec(memory_space=pltpu.SMEM)] + [vmem] * 4,
        out_specs=[vmem] * 3,
        scratch_shapes=[
            pltpu.VMEM((16, HALF, B), bf), pltpu.VMEM((4, 4, HALF, B), bf), pltpu.VMEM((4, 4, HALF, B), bf),
            pltpu.VMEM((2, 2, HALF, B), bf), pltpu.VMEM((4, HALF, B), bf), pltpu.VMEM((4, HALF, B), bf),
            pltpu.VMEM((2, HALF // 2, B), bf), pltpu.VMEM((16, HALF, B), bf), pltpu.VMEM((2, HALF, B), bf),
            pltpu.VMEM((8, 4, SLAB, B), bf), pltpu.VMEM((2, 4, SLAB, B), bf),
            pltpu.VMEM((2, 2, 2, SLAB, B), bf), pltpu.VMEM((2, 2, SLAB, B), bf),
            pltpu.VMEM((4, 2, 2, SLAB, B), bf), pltpu.VMEM((2, 2, SLAB, B), bf),
            pltpu.VMEM((4, 2, 2, SLAB, B), bf), pltpu.VMEM((2, 2, SLAB, B), bf), pltpu.VMEM((HALF, B), bf),
        ] + sems + sems,
        compiler_params=pltpu.CompilerParams(collective_id=0, has_side_effects=True, vmem_limit_bytes=24 * 2**20),
    )(pivots, colq, col63, rowq, row63)


def split_kernel(piv_ref, m_ref, d_ref, colq_ref, col63_ref, rowq_ref, row63_ref):
    group = pl.program_id(0)
    other = jnp.where(piv_ref[0] == 63, piv_ref[1], piv_ref[0])
    out_row = lax.broadcasted_iota(jnp.int32, (B, B), 0)
    in_row = lax.broadcasted_iota(jnp.int32, (B, B), 1)
    perm = jnp.where(in_row == (out_row % 64) * 4 + out_row // 64, 1.0, 0.0).astype(jnp.bfloat16)
    for r in range(2):
        for t in range(2):
            j = 2 * r + t
            parts = jnp.concatenate([m_ref[r, t, pl.ds(s * B, B), :] for s in range(4)], axis=1)
            sorted_rows = jnp.dot(perm, parts, preferred_element_type=jnp.float32).astype(jnp.bfloat16)
            for s in range(4):
                for lb in range(2):
                    for tc in range(2):
                        piece = sorted_rows[(lb * 2 + tc) * 64:(lb * 2 + tc + 1) * 64, s * 128:(s + 1) * 128]
                        lanes = pl.ds(lb * 128, 128)
                        d_ref[tc, group, j, pl.ds(s * 64, 64), lanes] = piece
                        if tc == 1:
                            col63_ref[8 * r + 2 * group + t, s // 2, pl.ds(s % 2 * 64, 64), lanes] = piece
            for h in range(2):
                colq_ref[8 * r + 2 * group + t, h] = d_ref[other // 32, group, j, pl.ds(h * HALF, HALF)]

            @pl.when(other // 8 == 2 * group + t)
            def _(r=r, j=j):
                for tc in range(2):
                    for w in range(8):
                        rowq_ref[w, 2 * tc + r] = d_ref[tc, group, j, pl.ds(w * SLAB, SLAB)]

            if t == 1:
                @pl.when(group == 3)
                def _(r=r, j=j):
                    for tc in range(2):
                        for w in range(8):
                            row63_ref[w, 2 * tc + r] = d_ref[tc, group, j, pl.ds(w * SLAB, SLAB)]


def split(pivots, packed):
    shape = jax.ShapeDtypeStruct
    vmem = pl.BlockSpec(memory_space=pltpu.VMEM)
    return pl.pallas_call(
        split_kernel,
        name="split",
        grid=(4,),
        out_shape=[
            shape((2, 4, 4, B, B), jnp.bfloat16),
            shape((16, 2, HALF, B), jnp.bfloat16),
            shape((16, 2, HALF, B), jnp.bfloat16),
            shape((8, 4, SLAB, B), jnp.bfloat16),
            shape((8, 4, SLAB, B), jnp.bfloat16),
        ],
        in_specs=[
            pl.BlockSpec(memory_space=pltpu.SMEM),
            pl.BlockSpec((2, 2, 4 * B, 128), lambda g: (0, g, 0, 0)),
        ],
        out_specs=[vmem] * 5,
        compiler_params=pltpu.CompilerParams(vmem_limit_bytes=24 * 2**20),
    )(pivots, packed)


def dot(left, right):
    return jnp.dot(left, right, preferred_element_type=jnp.float32)


def flat(pair):
    return jnp.concatenate([pair[0], pair[1]], axis=1)


def store_right(ref, pair, at=0, width=B):
    ref[pl.ds(0, B), pl.ds(at, B)] = pair[0]
    ref[pl.ds(B, B), pl.ds(at, B)] = -pair[1]
    ref[pl.ds(0, B), pl.ds(at + width, B)] = pair[1]
    ref[pl.ds(B, B), pl.ds(at + width, B)] = pair[0]


def halves(wide):
    return wide[:, :B], wide[:, B:]


def update_kernel(
    piv_ref, cl_ref, rl_ref, inv_ref, x_ref, u_ref, k_ref, d_ref, o_ref,
    f0, f1, rx0, rx1, rm01, ru0, ru1, tmp, l0, l1, tile,
):
    bf, f32 = jnp.bfloat16, jnp.float32
    group = pl.program_id(0)
    z = lax.axis_index("row")
    c = lax.axis_index("col")
    p0, p1 = piv_ref[0], piv_ref[1]
    s0 = jnp.where(p0 == 63, 1, 0)
    s1 = 1 - s0
    col_ids = [tc * 32 + c for tc in range(2)]
    cols0 = [(rl_ref[0, i] > 0) & (i != p0) for i in col_ids]
    cols1 = [(rl_ref[1, i] > 0) & (i != p0) & (i != p1) for i in col_ids]

    def from_column(s, r, row):
        return jnp.concatenate([x_ref[s, h, 2 * r + row // 4, row % 4] for h in range(2)], axis=0)

    def from_row(s, at):
        return jnp.concatenate([u_ref[w, s, at] for w in range(8)], axis=0)

    def corner(row, col):
        return [jnp.concatenate([k_ref[row, w, col, r] for w in range(8)], axis=0) for r in range(2)]

    def taken(row):
        return (cl_ref[0, row] > 0) & (row != p0), (cl_ref[1, row] > 0) & (row != p0) & (row != p1)

    @pl.when(group == 0)
    def _():
        def refine(diagonal, step, keep, keep_right, *meanwhile):
            guess = (inv_ref[step, 0], inv_ref[step, 1])
            store_right(tmp, guess)
            eye = lax.broadcasted_iota(jnp.int32, (B, B), 0) == lax.broadcasted_iota(jnp.int32, (B, B), 1)
            real, imag = halves(dot(diagonal, tmp[...]))
            if meanwhile:
                meanwhile[0]()
            store_right(tmp, ((jnp.where(eye, 2.0, 0.0) - real).astype(bf), (-imag).astype(bf)))
            keep[...] = dot(flat(guess), tmp[...]).astype(bf)
            if meanwhile:
                meanwhile[1]()
            store_right(keep_right, halves(keep[...]))

        def panel(s, q):
            return jnp.concatenate(
                [flat([from_column(s, r, 2 * q + t) for r in range(2)]) for t in range(2)], axis=0
            )

        def mixed(q, product, old, which):
            return jnp.concatenate(
                [
                    jnp.where(taken((2 * q + t) * 8 + z)[which], product[t * B:(t + 1) * B], old[t * B:(t + 1) * B])
                    for t in range(2)
                ],
                axis=0,
            ).astype(bf)

        def both(q):
            return pl.ds(2 * q * B, 2 * B)

        def first_panel(q):
            old = panel(s0, q)
            l0[both(q), :] = mixed(q, dot(old, rx0[...]), old.astype(f32), 0)

        def moved_panel(q):
            old = panel(s1, q).astype(f32)
            l1[both(q), :] = mixed(q, old - dot(l0[both(q), :], rm01[...]), old, 0)

        def second_panel(q):
            moved = l1[both(q), :]
            l1[both(q), :] = mixed(q, dot(moved, rx1[...]), moved.astype(f32), 1)

        store_right(rm01, corner(s0, s1))
        refine(flat(corner(s0, s0)), 0, f0, rx0)
        l10 = dot(flat(corner(s1, s0)), rx0[...]).astype(bf)
        first_panel(0)
        m11 = (flat(corner(s1, s1)).astype(f32) - dot(l10, rm01[...])).astype(bf)
        first_panel(1)
        refine(m11, 1, f1, rx1, lambda: (first_panel(2), first_panel(3)), lambda: (moved_panel(0), moved_panel(1)))
        for tc in range(2):
            store_right(ru0, (from_row(s0, 2 * tc), from_row(s0, 2 * tc + 1)), tc * B, 2 * B)
        product = dot(l10, ru0[...])
        for tc in range(2):
            pair = []
            for r in range(2):
                old = from_row(s1, 2 * tc + r).astype(f32)
                at = (2 * r + tc) * B
                pair.append(jnp.where(cols0[tc], old - product[:, at:at + B], old).astype(bf))
            store_right(ru1, pair, tc * B, 2 * B)

        moved_panel(2)
        moved_panel(3)
        for q in range(4):
            second_panel(q)

    first = dot(l0[pl.ds(4 * group * B, 4 * B), :], ru0[...])
    second = dot(l1[pl.ds(4 * group * B, 4 * B), :], ru1[...])
    for t in range(4):
        take0, take1 = taken((4 * group + t) * 8 + z)
        for tc in range(2):
            use0 = take0 & cols0[tc] & (col_ids[tc] != p1)
            use1 = take1 & cols1[tc]
            for r in range(2):
                old = d_ref[tc, 2 * group + t // 2, 2 * r + t % 2].astype(f32)
                at = (2 * r + tc) * B
                rows = slice(t * B, (t + 1) * B)
                old = jnp.where(use0, old - first[rows, at:at + B], old).astype(bf).astype(f32)
                tile[t, tc, r] = jnp.where(use1, old - second[rows, at:at + B], old).astype(bf)

    for tc in range(2):
        for pivot, left, factor in ((p0, l0, f0), (p1, l1, f1)):
            @pl.when(col_ids[tc] == pivot)
            def _(tc=tc, pivot=pivot, left=left, factor=factor):
                for t in range(4):
                    is_pivot = (4 * group + t) * 8 + z == pivot
                    for r in range(2):
                        lanes = pl.ds(r * B, B)
                        other = left[pl.ds((4 * group + t) * B, B), lanes].astype(f32)
                        tile[t, tc, r] = jnp.where(is_pivot, factor[:, lanes].astype(f32), other).astype(bf)

    out_row = lax.broadcasted_iota(jnp.int32, (B, B), 0)
    in_row = lax.broadcasted_iota(jnp.int32, (B, B), 1)
    perm = jnp.where(out_row == (in_row % 64) * 4 + in_row // 64, 1.0, 0.0).astype(bf)
    for t in range(4):
        for r in range(2):
            stacked = jnp.concatenate(
                [
                    jnp.concatenate(
                        [tile[t, tc, r, pl.ds(s * 64, 64), pl.ds(lb * 128, 128)] for s in range(4)], axis=1
                    )
                    for lb in range(2)
                    for tc in range(2)
                ],
                axis=0,
            )
            woven = dot(perm, stacked).astype(bf)
            for s in range(4):
                o_ref[r, t, pl.ds(s * B, B), :] = woven[:, s * 128:(s + 1) * 128]


def update(pivots, col_lists, row_lists, inverses, x, u, k, d):
    smem = pl.BlockSpec(memory_space=pltpu.SMEM)
    vmem_in = pl.BlockSpec(memory_space=pltpu.VMEM)
    square = pltpu.VMEM((2 * B, 2 * B), jnp.bfloat16)
    flat_square = pltpu.VMEM((B, 2 * B), jnp.bfloat16)
    wide = pltpu.VMEM((2 * B, 4 * B), jnp.bfloat16)
    panel = pltpu.VMEM((8 * B, 2 * B), jnp.bfloat16)
    return pl.pallas_call(
        update_kernel,
        name="update",
        grid=(2,),
        out_shape=jax.ShapeDtypeStruct((2, 8, 4 * B, 128), jnp.bfloat16),
        in_specs=[smem] * 3 + [vmem_in] * 5,
        out_specs=pl.BlockSpec((2, 4, 4 * B, 128), lambda g: (0, g, 0, 0)),
        scratch_shapes=[
            flat_square, flat_square, square, square, square, wide, wide, square, panel, panel,
            pltpu.VMEM((4, 2, 2, B, B), jnp.bfloat16),
        ],
        compiler_params=pltpu.CompilerParams(vmem_limit_bytes=32 * 2**20),
    )(pivots, col_lists, row_lists, inverses, x, u, k, d)


def shards(matrix, inverses, pivots, col_lists, row_lists):
    packed = matrix.reshape(2, 8, B, 2, 2, 128).transpose(0, 1, 2, 4, 3, 5).reshape(2, 8, 4 * B, 128)
    d, colq, col63, rowq, row63 = split(pivots, packed)
    x, u, k = gather(pivots, colq, col63, rowq, row63)
    out = update(pivots, col_lists, row_lists, inverses, x, u, k, d)
    return out.reshape(2, 8, B, 2, 2, 128).transpose(0, 1, 2, 4, 3, 5).reshape(matrix.shape)


def solution(mesh):
    tiled = P(None, None, "row", None, None, "col", None)
    return jax.shard_map(shards, mesh=mesh, in_specs=(tiled, P(), P(), P(), P()), out_specs=tiled, check_vma=False)
```
